512 devices in a mesh: slide: 16 (over z), ctx: 32 (over y, x, core).
Axes of the slice: x: 4, y: 4, z: 16, core: 2. Of those that a mesh axis runs over, the one named last changes fastest.
Arguments:
- tiles: bfloat16 [16, 16384, 768], P('slide', 'ctx'), may hold values from -40 to 40
- tile_pos: int32 [16, 16384], P('slide', 'ctx'), may hold values from 0 to 16383, as said below
- lengths: int32 [16], P('slide'), may hold values from 4096 to 16384, as said below
- qkv_weight: bfloat16 [768, 1152], replicated, may hold values from -0.21875 to 0.21875
- out_weight: bfloat16 [384, 768], replicated, may hold values from -0.3125 to 0.3125
- cotangent: bfloat16 [16, 16384, 768], P('slide', 'ctx'), may hold values from -6 to 6
Outputs:
- tile_grads: bfloat16 [16, 16384, 768], P('slide', 'ctx')
- out_weight_grad: float32 [294912], P(('slide', 'ctx'))
- far_kv_grads: float32 [16, 2, 6, 1024, 64], P('slide', None, None, 'ctx')
The draws below stay inside these ranges and needn't reach their ends.
Inputs may be any that keep to these rules, and one draw needn't show every extreme that they name: `tile_pos`: for every slide the entries are a permutation of its 16384 positions; the 512 entries held by one device of ctx contain exactly 16 positions of each block of 512 consecutive positions, in no particular order. `lengths`: at least one slide has all 16384 positions live.
All inputs are finite; a program needn't handle non-finite values.
Results may differ from the reference program's by a relative error of at most 0.014.
The reference program's roundings to bfloat16 on the way count: a program that leaves them out, or rounds other values in their place, can miss the bound.
Values may be sent and summed in bfloat16 or wider, within the bound.
No kernel may reach another device: no remote copies, remote signals or barrier semaphores. Data moves between devices by JAX's collectives and lax.ppermute only.
A program may use at most 128 MiB of HBM per device.

```python
import math
import jax
import jax.numpy as jnp
from jax import lax

D = 768
HEAD_COUNT = 6
HD = 64
WIDE_RATE2 = 16
TOK_DEV = 512
SLOT_COUNT = 16384
SLIDES = 16
PORTION = 16
N_CTX = 32


def draw_tiles(key, part):
    key = jax.random.fold_in(key, 5)
    first = jax.random.fold_in(key, 0)
    values = jax.random.normal(first, (SLIDES, SLOT_COUNT, D), jnp.float32)
    return jnp.clip(values, -40.0, 40.0).astype(jnp.bfloat16)


def shuffle_one(subkey):
    return jax.random.permutation(subkey, TOK_DEV).astype(jnp.int32)


def draw_tile_pos(key, part):
    key = jax.random.fold_in(key, 11)
    first, second = jax.random.split(key, 2)
    within = jax.vmap(shuffle_one)(jax.random.split(first, SLIDES * N_CTX)).reshape(SLIDES, N_CTX, TOK_DEV)
    within = within + (jnp.arange(N_CTX, dtype=jnp.int32) * TOK_DEV)[None, :, None]
    grouped = within.reshape(SLIDES, N_CTX, N_CTX, PORTION).transpose(0, 2, 1, 3).reshape(SLIDES, N_CTX, TOK_DEV)
    holder = jax.vmap(shuffle_one)(jax.random.split(second, SLIDES * N_CTX)).reshape(SLIDES, N_CTX, TOK_DEV)
    placed = jnp.take_along_axis(grouped, holder, -1)
    return placed.reshape(SLIDES, SLOT_COUNT).astype(jnp.int32)


def draw_lengths(key, part):
    key = jax.random.fold_in(key, 7)
    first, second = jax.random.split(key, 2)
    drawn = jax.random.randint(first, (SLIDES,), SLOT_COUNT // 4, SLOT_COUNT + 1, jnp.int32)
    picked = jax.random.randint(second, (), 0, SLIDES, jnp.int32)
    return jnp.where(jnp.arange(SLIDES) == picked, SLOT_COUNT, drawn).astype(jnp.int32)


def shard_levels(key, dims, cuts, smallest, largest):
    gain = 1.0
    for position, shards_of in cuts:
        steps = jax.random.uniform(jax.random.fold_in(jax.random.fold_in(key, 6), position), (shards_of,), jnp.float32, smallest / len(cuts), largest / len(cuts))
        gain = gain * jnp.repeat(jnp.exp(steps), dims[position] // shards_of).reshape((-1,) + (1,) * (len(dims) - 1 - position))
    return gain


def scatter_about(stream_key, extent, width, reach, pieces=(), kind=jnp.bfloat16):
    values = jax.random.normal(stream_key, extent, jnp.float32) * width
    if len(pieces) > 0:
        values = shard_levels(stream_key, extent, pieces, -0.22, 0.18) * values
    return jnp.clip(values, min=-reach, max=reach).astype(kind)


def setup_inputs(seed: int = 0) -> dict:
    streams_of = jax.random.split(jax.random.key(seed), 7)
    tiles = draw_tiles(jax.random.fold_in(streams_of[6], 71), 0)
    tile_pos = draw_tile_pos(jax.random.fold_in(streams_of[6], 71), 0)
    lengths = draw_lengths(jax.random.fold_in(streams_of[6], 71), 0)
    qkv_weight = scatter_about(streams_of[3], (D, 3 * HEAD_COUNT * HD), D ** -0.5, 0.21875)
    out_weight = scatter_about(streams_of[4], (HEAD_COUNT * HD, D), (HEAD_COUNT * HD) ** -0.5, 0.3125)
    cotangent = scatter_about(streams_of[5], (SLIDES, SLOT_COUNT, D), 1.0, 6.0, ((0, 16), (1, 32)))
    return dict(tiles=tiles, tile_pos=tile_pos, lengths=lengths, qkv_weight=qkv_weight, out_weight=out_weight, cotangent=cotangent)


NEGATIVE_FLOOR = -1e+30

def dilate(tensor, stride):
    number = tensor.shape[1]
    lattice = tensor.reshape(tensor.shape[0] // stride, stride, number, tensor.shape[2])
    return jnp.stack([lattice[:, offset, offset, :] for offset in range(number)], 0)

def selector(number, stride):
    return jnp.arange(stride)[None, :] == jnp.arange(number)[:, None]

def spread(values, stride, filler):
    chosen = selector(values.shape[0], stride)
    return jnp.where(chosen[:, None, :], values[:, :, None], filler).reshape(values.shape[0], -1)

def spread_rows(values, stride):
    chosen = selector(values.shape[0], stride)
    placed = jnp.where(chosen[:, None, :, None], values[:, :, None, :], 0.0)
    return placed.reshape(values.shape[0], -1, values.shape[2])

def extract(field, stride):
    chosen = selector(field.shape[0], stride)
    lattice = field.reshape(field.shape[0], -1, stride)
    return lax.optimization_barrier(jnp.sum(jnp.where(chosen[:, None, :], lattice, 0.0), -1))

def extract_rows(field, stride):
    chosen = selector(field.shape[0], stride)
    lattice = field.reshape(field.shape[0], -1, stride, field.shape[2])
    return lax.optimization_barrier(jnp.sum(jnp.where(chosen[:, None, :, None], lattice, 0.0), 2))

def rounded(values):
    return lax.optimization_barrier(values.astype(jnp.bfloat16)).astype(jnp.float32)

def by_heads(values, segments):
    return values.transpose(1, 0, 2, 3).reshape(HEAD_COUNT, SLOT_COUNT, HD)

def slide_pass(sequence, grad_seq, slide_length, qkv_weight, out_weight):
    segments = SLOT_COUNT // TOK_DEV
    projected = jnp.dot(sequence, qkv_weight, preferred_element_type=jnp.float32)
    projected = rounded(projected).reshape(SLOT_COUNT, 3, HEAD_COUNT, HD)
    queries = projected[:, 0]
    keyset = projected[:, 1]
    values = projected[:, 2]
    live_rows = jnp.arange(SLOT_COUNT) < slide_length
    seg_query = queries.reshape(segments, TOK_DEV, HEAD_COUNT, HD)
    seg_keys = keyset.reshape(segments, TOK_DEV, HEAD_COUNT, HD)
    seg_values = values.reshape(segments, TOK_DEV, HEAD_COUNT, HD)
    seg_live = live_rows.reshape(segments, 1, 1, TOK_DEV)
    local_scores = jnp.einsum('nqhd,nkhd->nhqk', seg_query, seg_keys) * 0.125
    local_masked = jnp.where(seg_live, local_scores, NEGATIVE_FLOOR)
    local_max = lax.optimization_barrier(jnp.max(local_masked, -1)).transpose(1, 0, 2).reshape(HEAD_COUNT, SLOT_COUNT)
    near_query = dilate(queries, WIDE_RATE2)
    near_keys = dilate(keyset, WIDE_RATE2)
    near_values = dilate(values, WIDE_RATE2)
    dilated_positions = jnp.arange(SLOT_COUNT // WIDE_RATE2)[None, :] * WIDE_RATE2 + jnp.arange(HEAD_COUNT)[:, None]
    dilated_live_mask = dilated_positions < slide_length
    distant_scores = jnp.einsum('hqd,hkd->hqk', near_query, near_keys) * 0.125
    distant_masked = jnp.where(dilated_live_mask[:, None, :], distant_scores, NEGATIVE_FLOOR)
    far_max = lax.optimization_barrier(jnp.max(distant_masked, -1))
    ceiling = jnp.maximum(local_max, spread(far_max, WIDE_RATE2, NEGATIVE_FLOOR))
    seg_ceiling = ceiling.reshape(HEAD_COUNT, segments, TOK_DEV).transpose(1, 0, 2)
    local_weights = jnp.where(seg_live, jnp.exp(local_masked - seg_ceiling[..., None]), 0.0)
    distant_ceiling = extract(ceiling, WIDE_RATE2)
    distant_weights = jnp.where(dilated_live_mask[:, None, :], jnp.exp(distant_masked - distant_ceiling[:, :, None]), 0.0)
    local_sums = lax.optimization_barrier(jnp.sum(local_weights, -1)).transpose(1, 0, 2).reshape(HEAD_COUNT, SLOT_COUNT)
    totals = local_sums + spread(lax.optimization_barrier(jnp.sum(distant_weights, -1)), WIDE_RATE2, 0.0)
    local_numer = by_heads(jnp.einsum('nhqk,nkhd->nhqd', rounded(local_weights), seg_values), segments)
    numerator = local_numer + spread_rows(jnp.einsum('hqk,hkd->hqd', rounded(distant_weights), near_values), WIDE_RATE2)
    divisor = jnp.where(live_rows[None, :], totals, 1.0)
    result = jnp.where(live_rows[None, :, None], numerator / divisor[:, :, None], 0.0)
    attention = result.transpose(1, 0, 2).reshape(SLOT_COUNT, HEAD_COUNT * HD).astype(jnp.bfloat16)
    partial_term = jnp.dot(attention.T, grad_seq, preferred_element_type=jnp.float32)
    grad_attn = jnp.dot(grad_seq, out_weight.T, preferred_element_type=jnp.float32)
    grad_attn = rounded(grad_attn).reshape(SLOT_COUNT, HEAD_COUNT, HD)
    grad_out = jnp.where(live_rows[:, None, None], grad_attn, 0.0).transpose(1, 0, 2)
    inner_stat = lax.optimization_barrier(jnp.sum(grad_out * result, -1))
    seg_divisor = divisor.reshape(HEAD_COUNT, segments, TOK_DEV).transpose(1, 0, 2)
    seg_stat = inner_stat.reshape(HEAD_COUNT, segments, TOK_DEV).transpose(1, 0, 2)
    seg_grad = grad_out.reshape(HEAD_COUNT, segments, TOK_DEV, HD).transpose(1, 0, 2, 3)
    local_prob = local_weights / seg_divisor[..., None]
    local_dprob = jnp.einsum('nhqd,nkhd->nhqk', seg_grad, seg_values)
    local_dscore = rounded(local_prob * (local_dprob - seg_stat[..., None]) * 0.125)
    grad_query = by_heads(jnp.einsum('nhqk,nkhd->nhqd', local_dscore, seg_keys), segments)
    grad_key = by_heads(jnp.einsum('nhqk,nqhd->nhkd', local_dscore, seg_query), segments)
    grad_value = by_heads(jnp.einsum('nhqk,nhqd->nhkd', rounded(local_prob), seg_grad), segments)
    near_divisor = extract(divisor, WIDE_RATE2)
    near_stat = extract(inner_stat, WIDE_RATE2)
    near_grad = extract_rows(grad_out, WIDE_RATE2)
    far_prob = distant_weights / near_divisor[:, :, None]
    far_dprob = jnp.einsum('hqd,hkd->hqk', near_grad, near_values)
    far_dscore = rounded(far_prob * (far_dprob - near_stat[:, :, None]) * 0.125)
    far_kgrad = jnp.einsum('hqk,hqd->hkd', far_dscore, near_query)
    far_vgrad = jnp.einsum('hqk,hqd->hkd', rounded(far_prob), near_grad)
    grad_query = grad_query + spread_rows(jnp.einsum('hqk,hkd->hqd', far_dscore, near_keys), WIDE_RATE2)
    grad_key = grad_key + spread_rows(far_kgrad, WIDE_RATE2)
    grad_value = grad_value + spread_rows(far_vgrad, WIDE_RATE2)
    far_pair = jnp.stack([far_kgrad, far_vgrad], 0) * math.sqrt(SLOT_COUNT // WIDE_RATE2)
    stacked = jnp.stack([grad_query, grad_key, grad_value], 0).transpose(2, 0, 1, 3)
    stacked = stacked.reshape(SLOT_COUNT, 3 * HEAD_COUNT * HD).astype(jnp.bfloat16)
    grad_tiles = jnp.dot(stacked, qkv_weight.T, preferred_element_type=jnp.float32).astype(jnp.bfloat16)
    return (grad_tiles, partial_term, far_pair)

def reference(tiles, tile_pos, lengths, qkv_weight, out_weight, cotangent):

    def one_slide(bundle):
        owned, places, slide_length, grad_seq = bundle
        sequence = jnp.zeros_like(owned).at[places].set(owned)
        grad_tiles, partial_term, far_pair = slide_pass(sequence, grad_seq, slide_length, qkv_weight, out_weight)
        return (grad_tiles[places], partial_term, far_pair)
    backs, terms, far_pairs = lax.map(one_slide, (tiles, tile_pos, lengths, cotangent))
    factor = 1.0 / math.sqrt(SLIDES * SLOT_COUNT)
    weight_grad = lax.optimization_barrier(jnp.sum(terms * factor, 0)).reshape(-1)
    return (backs, weight_grad, far_pairs.astype(jnp.float32))
```

```python
import math

import jax
import jax.numpy as jnp
from jax import lax
from jax.sharding import PartitionSpec as P

HD = 64
WIDE_RATE2 = 16


NEGATIVE_FLOOR = -1e30


def dilate(tensor, stride):
    number = tensor.shape[1]
    lattice = tensor.reshape(tensor.shape[0] // stride, stride, number, tensor.shape[2])
    return jnp.stack([lattice[:, offset, offset, :] for offset in range(number)], 0)


def selector(number, stride):
    return jnp.arange(stride)[None, :] == jnp.arange(number)[:, None]


def spread(values, stride, filler):
    chosen = selector(values.shape[0], stride)
    return jnp.where(chosen[:, None, :], values[:, :, None], filler).reshape(values.shape[0], -1)


def spread_rows(values, stride):
    chosen = selector(values.shape[0], stride)
    placed = jnp.where(chosen[:, None, :, None], values[:, :, None, :], 0.0)
    return placed.reshape(values.shape[0], -1, values.shape[2])


def extract(field, stride):
    chosen = selector(field.shape[0], stride)
    lattice = field.reshape(field.shape[0], -1, stride)
    return jnp.sum(jnp.where(chosen[:, None, :], lattice, 0.0), -1)


def extract_rows(field, stride):
    chosen = selector(field.shape[0], stride)
    lattice = field.reshape(field.shape[0], -1, stride, field.shape[2])
    return jnp.sum(jnp.where(chosen[:, None, :, None], lattice, 0.0), 2)


def local(tiles, tile_pos, lengths, qkv_weight, out_weight, cotangent):
    row_count = tiles.shape[1]
    features = tiles.shape[2]
    peer_count = lax.axis_size("ctx")
    device = lax.axis_index("ctx")
    portion = row_count // peer_count
    number = out_weight.shape[0] // HD
    stride = WIDE_RATE2
    groups = row_count // stride
    places = tile_pos[0]
    ordering = jnp.argsort(places // row_count, stable=True)
    sent_rows = tiles[0][ordering].reshape(peer_count, portion, features)
    sent_places = places[ordering].reshape(peer_count, portion)
    got_rows, got_places = (
        lax.all_to_all(sent_rows, "ctx", split_axis=0, concat_axis=0, tiled=True),
        lax.all_to_all(sent_places, "ctx", split_axis=0, concat_axis=0, tiled=True),
    )
    slot_index = got_places.reshape(row_count) - device * row_count
    sequence = (
        jnp.zeros((row_count, features), jnp.bfloat16)
        .at[slot_index]
        .set(got_rows.reshape(row_count, features))
    )
    projected = jnp.dot(sequence, qkv_weight, preferred_element_type=jnp.float32).astype(
        jnp.bfloat16
    )
    projected = projected.reshape(row_count, 3, number, HD)
    queries = projected[:, 0]
    keyset = projected[:, 1]
    values = projected[:, 2]
    slide_length = lengths[0]
    live_rows = device * row_count + jnp.arange(row_count) < slide_length
    local_scores = (
        jnp.einsum("qhd,khd->hqk", queries, keyset, preferred_element_type=jnp.float32) * 0.125
    )
    local_masked = jnp.where(live_rows[None, None, :], local_scores, NEGATIVE_FLOOR)
    local_max = jnp.max(local_masked, -1)
    near_query = dilate(queries, stride)
    near_keys = dilate(keyset, stride)
    near_values = dilate(values, stride)
    far_keys, far_values = (
        lax.all_gather(near_keys, "ctx", axis=1, tiled=True),
        lax.all_gather(near_values, "ctx", axis=1, tiled=True),
    )
    head_offsets = jnp.arange(number)[:, None]
    far_live = jnp.arange(groups * peer_count)[None, :] * stride + head_offsets < slide_length
    distant_scores = (
        jnp.einsum("hqd,hkd->hqk", near_query, far_keys, preferred_element_type=jnp.float32) * 0.125
    )
    distant_masked = jnp.where(far_live[:, None, :], distant_scores, NEGATIVE_FLOOR)
    far_max = jnp.max(distant_masked, -1)
    ceiling = jnp.maximum(local_max, spread(far_max, stride, NEGATIVE_FLOOR))
    local_weights = jnp.where(
        live_rows[None, None, :], jnp.exp(local_masked - ceiling[:, :, None]), 0.0
    )
    distant_ceiling = extract(ceiling, stride)
    distant_weights = jnp.where(
        far_live[:, None, :], jnp.exp(distant_masked - distant_ceiling[:, :, None]), 0.0
    )
    totals = jnp.sum(local_weights, -1) + spread(jnp.sum(distant_weights, -1), stride, 0.0)
    local_numer = jnp.einsum(
        "hqk,khd->hqd",
        local_weights.astype(jnp.bfloat16),
        values,
        preferred_element_type=jnp.float32,
    )
    far_numer = jnp.einsum(
        "hqk,hkd->hqd",
        distant_weights.astype(jnp.bfloat16),
        far_values,
        preferred_element_type=jnp.float32,
    )
    numerator = local_numer + spread_rows(far_numer, stride)
    divisor = jnp.where(live_rows[None, :], totals, 1.0)
    result = jnp.where(live_rows[None, :, None], numerator / divisor[:, :, None], 0.0)
    attention = result.transpose(1, 0, 2).reshape(row_count, number * HD).astype(jnp.bfloat16)
    grad_seq = cotangent[0]
    factor = 1.0 / math.sqrt(lax.axis_size("slide") * peer_count * row_count)
    partial_term = (
        jnp.einsum("qc,qd->cd", attention, grad_seq, preferred_element_type=jnp.float32) * factor
    )
    slides = lax.axis_size("slide")
    pieces = partial_term.astype(jnp.bfloat16).reshape(slides, peer_count, -1).transpose(1, 0, 2)
    pieces = lax.all_to_all(pieces, "ctx", split_axis=0, concat_axis=0, tiled=True)
    pieces = jnp.sum(pieces.astype(jnp.float32), 0)
    pieces = lax.all_to_all(pieces, "slide", split_axis=0, concat_axis=0, tiled=True)
    weight_grad = jnp.sum(pieces, 0)
    grad_attn = jnp.einsum(
        "qd,cd->qc", grad_seq, out_weight, preferred_element_type=jnp.float32
    ).astype(jnp.bfloat16)
    grad_attn = grad_attn.reshape(row_count, number, HD)
    grad_out = jnp.where(
        live_rows[:, None, None], grad_attn, jnp.zeros((), jnp.bfloat16)
    ).transpose(1, 0, 2)
    inner_stat = jnp.sum(grad_out.astype(jnp.float32) * result, -1)
    local_prob = local_weights / divisor[:, :, None]
    local_dprob = jnp.einsum("hqd,khd->hqk", grad_out, values, preferred_element_type=jnp.float32)
    local_dscore = (local_prob * (local_dprob - inner_stat[:, :, None]) * 0.125).astype(
        jnp.bfloat16
    )
    grad_query = jnp.einsum(
        "hqk,khd->hqd", local_dscore, keyset, preferred_element_type=jnp.float32
    )
    grad_key = jnp.einsum("hqk,qhd->hkd", local_dscore, queries, preferred_element_type=jnp.float32)
    grad_value = jnp.einsum(
        "hqk,hqd->hkd",
        local_prob.astype(jnp.bfloat16),
        grad_out,
        preferred_element_type=jnp.float32,
    )
    near_divisor = extract(divisor, stride)
    near_stat = extract(inner_stat, stride)
    near_grad = extract_rows(grad_out.astype(jnp.float32), stride).astype(jnp.bfloat16)
    far_prob = distant_weights / near_divisor[:, :, None]
    far_dprob = jnp.einsum(
        "hqd,hkd->hqk", near_grad, far_values, preferred_element_type=jnp.float32
    )
    far_dscore = (far_prob * (far_dprob - near_stat[:, :, None]) * 0.125).astype(jnp.bfloat16)
    far_qgrad = jnp.einsum("hqk,hkd->hqd", far_dscore, far_keys, preferred_element_type=jnp.float32)
    grad_query = grad_query + spread_rows(far_qgrad, stride)
    partial_keys = jnp.einsum(
        "hqk,hqd->hkd", far_dscore, near_query, preferred_element_type=jnp.float32
    )
    partial_values = jnp.einsum(
        "hqk,hqd->hkd", far_prob.astype(jnp.bfloat16), near_grad, preferred_element_type=jnp.float32
    )
    pair = jnp.stack([partial_keys, partial_values], 0).astype(jnp.bfloat16)
    pair = pair.reshape(2 * number, peer_count, groups, HD).transpose(1, 0, 2, 3)
    pair = lax.all_to_all(pair, "ctx", split_axis=0, concat_axis=0, tiled=True)
    pair = jnp.sum(pair.astype(jnp.float32), 0).reshape(2, number, groups, HD)
    owned_kgrad, owned_vgrad = pair[0], pair[1]
    grad_key = grad_key + spread_rows(owned_kgrad, stride)
    grad_value = grad_value + spread_rows(owned_vgrad, stride)
    far_pair = jnp.stack([owned_kgrad, owned_vgrad], 0) * math.sqrt(groups * peer_count)
    stacked = jnp.stack([grad_query, grad_key, grad_value], 0).transpose(2, 0, 1, 3)
    stacked = stacked.reshape(row_count, 3 * number * HD).astype(jnp.bfloat16)
    grad_rows = jnp.einsum(
        "qc,dc->qd", stacked, qkv_weight, preferred_element_type=jnp.float32
    ).astype(jnp.bfloat16)
    back_rows = grad_rows[slot_index].reshape(peer_count, portion, features)
    returned = lax.all_to_all(back_rows, "ctx", split_axis=0, concat_axis=0, tiled=True)
    tile_grads = (
        jnp.zeros((row_count, features), jnp.bfloat16)
        .at[ordering]
        .set(returned.reshape(row_count, features))
    )
    return (tile_grads[None], weight_grad, far_pair[None])


def solution(mesh):
    placed = (
        P("slide", "ctx", None),
        P("slide", "ctx"),
        P("slide"),
        P(),
        P(),
        P("slide", "ctx", None),
    )
    return jax.shard_map(
        local,
        mesh=mesh,
        in_specs=placed,
        out_specs=(
            P("slide", "ctx", None),
            P(("slide", "ctx")),
            P("slide", None, None, "ctx", None),
        ),
        check_vma=False,
    )
```

```python
import math

import jax
import jax.numpy as jnp
from jax import lax
from jax.experimental import pallas as pl
from jax.experimental.pallas import tpu as pltpu
from jax.sharding import PartitionSpec as P

HD = 64
HEADS = 6
STRIDE = 16
PEERS = 32
ROWS = 512
PORTION = 16
GROUPS = ROWS // STRIDE
FAR = HEADS * GROUPS
WIDTH = 768
INNER = HEADS * HD
QUERIES = 8 * GROUPS
KEYS = PEERS * GROUPS
CHUNK = GROUPS + 8
PIECE = 640
FLOOR = -1e30
SCALE = 0.125
LOG_SCALE = 0.125 * math.log2(math.e)
BF = jnp.bfloat16
F32 = jnp.float32


def nn(a, b):
    return lax.dot_general(a, b, (((1,), (0,)), ((), ())), preferred_element_type=F32)


def nt(a, b):
    return lax.dot_general(a, b, (((1,), (1,)), ((), ())), preferred_element_type=F32)


def tn(a, b):
    return lax.dot_general(a, b, (((0,), (0,)), ((), ())), preferred_element_type=F32)


def iota(shape, dim):
    return lax.broadcasted_iota(jnp.int32, shape, dim)


def mark(mask):
    return jnp.where(mask, 1.0, 0.0).astype(BF)


def split3(x):
    high = x.astype(BF)
    rest = x - high.astype(F32)
    middle = rest.astype(BF)
    low = (rest - middle.astype(F32)).astype(BF)
    return high.astype(F32), middle.astype(F32), low.astype(F32)


def key_bias(count, live):
    return jnp.where(iota((1, count), 1) < live, 0.0, FLOOR)


def far_rows():
    r = iota((FAR, ROWS), 0)
    return mark(((r & (GROUPS - 1)) * STRIDE + (r >> 5)) == iota((FAR, ROWS), 1))


def own_head():
    return (iota((FAR, INNER), 0) >> 5) == (iota((FAR, INNER), 1) >> 6)


def fold(offset):
    return mark((iota((INNER, 128), 0) & (HD - 1)) + offset == iota((INNER, 128), 1))


def pack_kernel(pos_ref, tiles_ref, send_ref, slot_ref):
    places = pos_ref[...]
    block = places >> 9
    member = iota((PEERS, ROWS), 0) == block
    before = mark(iota((ROWS, ROWS), 0) < iota((ROWS, ROWS), 1))
    counts = nn(mark(member), before)
    rank = jnp.sum(jnp.where(member, counts, 0.0), 0, keepdims=True)
    slot = block * PORTION + rank.astype(jnp.int32)
    slot_ref[...] = slot
    order = mark(iota((ROWS, ROWS), 0) == slot)
    send_ref[:, :WIDTH] = nn(order, tiles_ref[...]).astype(BF)
    inside = places & (ROWS - 1)
    line = iota((128, ROWS), 0)
    code = jnp.where(line == 0, inside >> 4, jnp.where(line == 1, inside & 15, 0))
    send_ref[:, WIDTH:] = nt(order, code.astype(F32).astype(BF)).astype(BF)


def project_kernel(
    scal_ref, recv_ref, weight_ref, grad_ref, proj_ref, far_ref, fgrad_ref, mean_ref, lse_ref, send_ref
):
    lane = iota((8, 128), 1)
    pick = jnp.where(iota((8, 128), 0) == 0, jnp.where(lane == 0, 16.0, jnp.where(lane == 1, 1.0, 0.0)), 0.0)
    place = nt(pick.astype(BF), recv_ref[:, WIDTH:])[0:1].astype(jnp.int32)
    order = mark(iota((ROWS, ROWS), 0) == place)
    sequence = nn(order, recv_ref[:, :WIDTH]).astype(BF)
    proj = nn(sequence, weight_ref[...]).astype(BF)
    proj_ref[...] = proj
    chosen = far_rows()
    own = own_head()
    far = nn(chosen, proj)
    fq = jnp.where(own, far[:, :INNER], 0.0).astype(BF)
    fk = jnp.where(own, far[:, INNER : 2 * INNER], 0.0).astype(BF)
    fv = jnp.where(own, far[:, 2 * INNER :], 0.0).astype(BF)
    fgrad = jnp.where(own, nn(chosen, grad_ref[...]), 0.0).astype(BF)
    far_ref[...] = fq
    fgrad_ref[...] = fgrad
    scores = nt(fq, proj[:, INNER : 2 * INNER]) * LOG_SCALE + key_bias(ROWS, scal_ref[0])
    top = jnp.max(scores, -1, keepdims=True)
    weight = jnp.exp2(scores - top)
    total = jnp.sum(weight, -1, keepdims=True)
    mean = jnp.where(own, nn(weight.astype(BF), proj[:, 2 * INNER :]) / total, 0.0)
    mean_ref[...] = mean
    lse = top + jnp.log2(total)
    lse_ref[...] = jnp.broadcast_to(lse, (FAR, 128))
    inner = jnp.sum(fgrad.astype(F32) * mean, -1, keepdims=True)
    first, second = fold(0), fold(HD)
    key_value = (nn(fk, first) + nn(fv, second)).astype(BF)
    query_grad = (nn(fq, first) + nn(fgrad, second)).astype(BF)
    column = iota((FAR, 128), 1)
    stats = jnp.zeros((FAR, 128), F32)
    for at, part in enumerate(split3(lse) + split3(inner)):
        stats = jnp.where(column == at, part, stats)
    stats = jnp.concatenate([stats, jnp.zeros((QUERIES - FAR, 128), F32)], 0).astype(BF)
    stats = nt(mark(iota((8, 128), 0) == iota((8, 128), 1)), stats).astype(BF)
    for peer in range(PEERS):
        head = (peer % 8) % HEADS
        rows = slice(head * GROUPS, (head + 1) * GROUPS)
        send_ref[peer, :GROUPS, :128] = key_value[rows]
        send_ref[peer, :GROUPS, 128:] = query_grad[rows]
        send_ref[peer, GROUPS:, :] = stats


def local_kernel(scal_ref, q_ref, k_ref, v_ref, grad_ref, att_ref, dq_ref, dk_ref, dv_ref):
    pair = pl.program_id(0)
    live = scal_ref[0]
    bias = key_bias(ROWS, live)
    q, k, v, grad = q_ref[...], k_ref[...], v_ref[...], grad_ref[...]
    row = iota((ROWS, 128), 0)
    side = iota((ROWS, 128), 1) >> 6
    zero = jnp.zeros((), BF)
    atts, dqs, dks, dvs = [], [], [], []
    for half in range(2):
        ours = side == half
        kept = ours & ((row & (STRIDE - 1)) != pair * 2 + half)
        query = jnp.where(ours, q, zero)
        out_grad = jnp.where(kept, grad, zero)
        scores = nt(query, k) * LOG_SCALE + bias
        weight = jnp.exp2(scores - jnp.max(scores, -1, keepdims=True))
        inverse = 1.0 / jnp.sum(weight, -1, keepdims=True)
        result = jnp.where(kept & (row < live), nn(weight.astype(BF), v) * inverse, 0.0)
        stat = jnp.sum(out_grad.astype(F32) * result, -1, keepdims=True)
        prob = weight * inverse
        dscore = (prob * (nt(out_grad, v) - stat) * SCALE).astype(BF)
        atts.append(result)
        dqs.append(jnp.where(kept, nn(dscore, k), 0.0))
        dks.append(tn(dscore, query))
        dvs.append(tn(prob.astype(BF), out_grad))
    att_ref[...] = (atts[0] + atts[1]).astype(BF)
    dq_ref[...] = (dqs[0] + dqs[1]).astype(BF)
    dk_ref[...] = dks[0] + dks[1]
    dv_ref[...] = dvs[0] + dvs[1]


def far_kernel(scal_ref, recv_ref, send_ref):
    first = scal_ref[2] * 8
    head = scal_ref[3]
    kv = recv_ref[:, :GROUPS, :128].reshape(KEYS, 128)
    mine = recv_ref[pl.ds(first, 8), :GROUPS, 128:].reshape(QUERIES, 128)
    pick = mark(iota((GROUPS, QUERIES), 1) == iota((GROUPS, QUERIES), 0) + head * GROUPS)
    parts = [nt(pick, recv_ref[first + j, GROUPS:, :]) for j in range(8)]
    parts = jnp.concatenate(parts, 0)
    lse = parts[:, 0:1] + parts[:, 1:2] + parts[:, 2:3]
    inner = parts[:, 3:4] + parts[:, 4:5] + parts[:, 5:6]
    left = iota((QUERIES, 128), 1) < HD
    zero = jnp.zeros((), BF)
    query = jnp.where(left, mine, zero)
    grad = jnp.where(left, zero, mine)
    alive = iota((1, KEYS), 1) * STRIDE + head < scal_ref[1]
    scores = nt(query, kv) * LOG_SCALE + jnp.where(alive, 0.0, FLOOR)
    top = jnp.max(scores, -1, keepdims=True)
    weight = jnp.exp2(scores - top)
    ceiling = jnp.maximum(top, lse)
    gain = jnp.exp2(top - ceiling)
    near = jnp.exp2(lse - ceiling)
    inverse = 1.0 / (jnp.sum(weight, -1, keepdims=True) * gain + near)
    gain = gain * inverse
    share = near * inverse
    numerator = nn(weight.astype(BF), kv) * gain
    stat = jnp.sum(grad.astype(F32) * numerator, -1, keepdims=True) + share * inner
    prob = weight * gain
    dscore = (prob * (nt(grad, kv) - stat) * SCALE).astype(BF)
    query_out = jnp.where(left, nn(dscore, kv), numerator).astype(BF)
    key_left = iota((KEYS, 128), 1) < HD
    key_out = jnp.where(key_left, tn(dscore, mine), tn(prob.astype(BF), mine)).astype(BF)
    column = iota((QUERIES, 128), 1)
    stats = jnp.zeros((QUERIES, 128), F32)
    for at, part in enumerate(split3(share)):
        stats = jnp.where(column == at, part, stats)
    stats = nt(mark(iota((8, 128), 0) == iota((8, 128), 1)), stats.astype(BF)).astype(BF)
    for peer in range(PEERS):
        j = peer % 8
        send_ref[peer, :GROUPS, :128] = key_out[peer * GROUPS : (peer + 1) * GROUPS]
        send_ref[peer, :GROUPS, 128:] = query_out[j * GROUPS : (j + 1) * GROUPS]
        send_ref[peer, GROUPS:, :] = stats


def returned_far(scal_ref, recv_ref):
    first = scal_ref[2] * 8
    pick = mark(iota((GROUPS, QUERIES), 1) == iota((GROUPS, QUERIES), 0) + scal_ref[4] * GROUPS)
    shares = jnp.concatenate([nt(pick, recv_ref[first + h, GROUPS:, :]) for h in range(HEADS)], 0)
    share = shares[:, 0:1] + shares[:, 1:2] + shares[:, 2:3]
    query_out = jnp.concatenate([recv_ref[first + h, :GROUPS, 128:] for h in range(HEADS)], 0)
    return share, query_out


def far_result(scal_ref, share, query_out, mean):
    r = iota((FAR, INNER), 0)
    live = (r & (GROUPS - 1)) * STRIDE + (r >> 5) < scal_ref[0]
    numerator = nt(query_out, fold(HD))
    return jnp.where(live & own_head(), numerator + share * mean, 0.0)


def weight_kernel(scal_ref, recv_ref, mean_ref, att_ref, cot_ref, send_ref):
    share, query_out = returned_far(scal_ref, recv_ref)
    result = far_result(scal_ref, share, query_out, mean_ref[...]).astype(BF)
    attention = att_ref[...] + tn(far_rows(), result).astype(BF)
    new = iota((INNER, INNER), 1)
    old = 3 * (8 * (new & 15) + ((new >> 4) & 7)) + (new >> 7)
    attention = nn(attention, mark(iota((INNER, INNER), 0) == old)).astype(BF)
    terms = (tn(attention, cot_ref[...]) * (1.0 / 512.0)).astype(BF)
    one, two, three = terms[:128], terms[128:256], terms[256:]
    pieces = (
        one[:, :PIECE],
        jnp.concatenate([one[:, 512:], two[:, :384]], 1),
        jnp.concatenate([two[:, 384:], three[:, :256]], 1),
        three[:, 128:],
    )
    for r in range(4):
        for q in range(8):
            send_ref[4 * q + r] = pieces[r][16 * q : 16 * q + 16]


def finish_kernel(
    scal_ref,
    recv_ref,
    proj_ref,
    far_ref,
    fgrad_ref,
    mean_ref,
    lse_ref,
    dq_ref,
    dk_ref,
    dv_ref,
    weight_ref,
    code_ref,
    back_ref,
    pair_ref,
):
    share, query_out = returned_far(scal_ref, recv_ref)
    result = far_result(scal_ref, share, query_out, mean_ref[...])
    fq, fgrad = far_ref[...], fgrad_ref[...]
    keys, values = proj_ref[:, INNER : 2 * INNER], proj_ref[:, 2 * INNER :]
    stat = jnp.sum(fgrad.astype(F32) * result, -1, keepdims=True)
    scores = nt(fq, keys) * LOG_SCALE + key_bias(ROWS, scal_ref[0])
    prob = jnp.exp2(scores - lse_ref[:, 0:1]) * share
    dscore = (prob * (nt(fgrad, values) - stat) * SCALE).astype(BF)
    own = own_head()
    chosen = far_rows()
    far_dq = jnp.where(own, nn(dscore, keys) + nt(query_out, fold(0)), 0.0).astype(BF)
    pairs = []
    for h in range(HEADS):
        total = recv_ref[h, :GROUPS, :128].astype(F32)
        for b in range(1, 4):
            total = total + recv_ref[8 * b + h, :GROUPS, :128].astype(F32)
        pairs.append(total)
    pairs = jnp.concatenate(pairs, 0)
    scaled = pairs * 32.0
    pair_ref[0] = scaled[:, :HD]
    pair_ref[1] = scaled[:, HD:]
    high = pairs.astype(BF)
    low = (pairs - high.astype(F32)).astype(BF)
    zero = jnp.zeros((), F32)

    def placed(offset):
        table = fold(offset)
        upper = jnp.where(own, nt(high, table), zero).astype(BF)
        lower = jnp.where(own, nt(low, table), zero).astype(BF)
        return tn(chosen, upper) + tn(chosen, lower)

    grad_query = dq_ref[...] + tn(chosen, far_dq).astype(BF)
    grad_key = (dk_ref[...] + tn(dscore, fq) + placed(0)).astype(BF)
    grad_value = (dv_ref[...] + tn(prob.astype(BF), fgrad) + placed(HD)).astype(BF)
    rows = nt(grad_query, weight_ref[:, :INNER])
    rows = rows + nt(grad_key, weight_ref[:, INNER : 2 * INNER])
    rows = rows + nt(grad_value, weight_ref[:, 2 * INNER :])
    code = code_ref[...].astype(F32)
    place = (code[:, 0:1] * 16.0 + code[:, 1:2]).astype(jnp.int32)
    order = mark(iota((ROWS, ROWS), 1) == place)
    back_ref[...] = nn(order, rows.astype(BF)).astype(BF)


def unpack_kernel(slot_ref, rows_ref, out_ref):
    order = mark(iota((ROWS, ROWS), 0) == slot_ref[...])
    out_ref[...] = tn(order, rows_ref[...]).astype(BF)


def call(body, outs, flops, name, **rest):
    return pl.pallas_call(
        body,
        out_shape=outs,
        name=name,
        compiler_params=pltpu.CompilerParams(vmem_limit_bytes=40 * 1024 * 1024),
        cost_estimate=pl.CostEstimate(flops=flops, bytes_accessed=4_000_000, transcendentals=0),
        **rest,
    )


def shape(dims, dtype=BF):
    return jax.ShapeDtypeStruct(dims, dtype)


def exchange(rows, axis):
    return lax.all_to_all(rows, axis, split_axis=0, concat_axis=0, tiled=True)


SMEM = pl.BlockSpec(memory_space=pltpu.SMEM)
WHOLE = pl.BlockSpec(memory_space=pltpu.VMEM)


def local(tiles, tile_pos, lengths, qkv_weight, out_weight, cotangent):
    device = lax.axis_index("ctx")
    length = lengths[0]
    live = length - device * ROWS
    scal = jnp.stack([live, length, device // 8, (device % 8) % HEADS, device % 8]).astype(jnp.int32)
    cot = cotangent[0]

    sent, slot = call(pack_kernel, (shape((ROWS, 896)), shape((1, ROWS), jnp.int32)), 800_000_000, "pack")(
        tile_pos, tiles[0]
    )
    got = exchange(sent.reshape(PEERS, PORTION, 896), "ctx").reshape(ROWS, 896)

    grad_attn = jnp.einsum("qd,cd->qc", cot, out_weight, preferred_element_type=F32).astype(BF)
    alive = lax.broadcasted_iota(jnp.int32, (ROWS, 1), 0) < live
    grad_out = jnp.where(alive, grad_attn, jnp.zeros((), BF))

    proj, far_q, far_grad, mean, lse, far_sent = call(
        project_kernel,
        (
            shape((ROWS, 3 * INNER)),
            shape((FAR, INNER)),
            shape((FAR, INNER)),
            shape((FAR, INNER), F32),
            shape((FAR, 128), F32),
            shape((PEERS, CHUNK, 256)),
        ),
        3_000_000_000,
        "project",
        in_specs=[SMEM, WHOLE, WHOLE, WHOLE],
    )(scal, got, qkv_weight, grad_out)
    far_got = exchange(far_sent, "ctx")

    def columns(base):
        return pl.BlockSpec((ROWS, 128), lambda t: (0, base + t))

    att, dq, dk, dv = call(
        local_kernel,
        (shape((ROWS, INNER)), shape((ROWS, INNER)), shape((ROWS, INNER), F32), shape((ROWS, INNER), F32)),
        12_000_000_000,
        "local_rows",
        grid=(3,),
        in_specs=[SMEM, columns(0), columns(3), columns(6), columns(0)],
        out_specs=(columns(0),) * 4,
    )(scal, proj, proj, proj, grad_out)

    far_back = call(far_kernel, shape((PEERS, CHUNK, 256)), 3_000_000_000, "far", in_specs=[SMEM, WHOLE])(
        scal, far_got
    )
    far_back = exchange(far_back, "ctx")

    pieces = call(
        weight_kernel,
        shape((PEERS, 16, PIECE)),
        1_000_000_000,
        "weight",
        in_specs=[SMEM, WHOLE, WHOLE, WHOLE, WHOLE],
    )(scal, far_back, mean, att, cot)
    pieces = exchange(pieces, "ctx")
    pieces = jnp.sum(pieces.astype(F32), 0)
    pieces = exchange(pieces, "slide")
    pieces = jnp.sum(pieces, 0)
    weight_grad = lax.dynamic_slice(pieces, (HD * (device % 2),), (576,))

    back, pair = call(
        finish_kernel,
        (shape((ROWS, WIDTH)), shape((2, FAR, HD), F32)),
        4_000_000_000,
        "finish",
        grid=(1,),
        in_specs=[SMEM]
        + [pl.BlockSpec(s, lambda t, n=len(s): (0,) * n) for s in ((PEERS, CHUNK, 256), (ROWS, 3 * INNER))]
        + [pl.BlockSpec((FAR, INNER), lambda t: (0, 0))] * 3
        + [pl.BlockSpec((FAR, 128), lambda t: (0, 0))]
        + [pl.BlockSpec((ROWS, INNER), lambda t: (0, 0))] * 3
        + [pl.BlockSpec((WIDTH, 3 * INNER), lambda t: (0, 0)), pl.BlockSpec((ROWS, 128), lambda t: (0, 6))],
        out_specs=(
            pl.BlockSpec((ROWS, WIDTH), lambda t: (0, 0)),
            pl.BlockSpec((2, FAR, HD), lambda t: (0, 0, 0)),
        ),
    )(scal, far_back, proj, far_q, far_grad, mean, lse, dq, dk, dv, qkv_weight, got)
    returned = exchange(back.reshape(PEERS, PORTION, WIDTH), "ctx").reshape(ROWS, WIDTH)
    tile_grads = call(unpack_kernel, shape((ROWS, WIDTH)), 400_000_000, "unpack")(slot, returned)
    return (tile_grads[None], weight_grad, pair.reshape(1, 2, HEADS, GROUPS, HD))


def solution(mesh):
    placed = (
        P("slide", "ctx", None),
        P("slide", "ctx"),
        P("slide"),
        P(),
        P(),
        P("slide", "ctx", None),
    )
    return jax.shard_map(
        local,
        mesh=mesh,
        in_specs=placed,
        out_specs=(
            P("slide", "ctx", None),
            P(("slide", "ctx")),
            P("slide", None, None, "ctx", None),
        ),
        check_vma=False,
    )
```

```python
import math

import jax
import jax.numpy as jnp
from jax import lax
from jax.experimental import pallas as pl
from jax.experimental.pallas import tpu as pltpu
from jax.sharding import PartitionSpec as P

HD = 64
HEADS = 6
STRIDE = 16
PEERS = 32
ROWS = 512
PORTION = 16
GROUPS = ROWS // STRIDE
FAR = HEADS * GROUPS
WIDTH = 768
INNER = HEADS * HD
QUERIES = 8 * GROUPS
KEYS = PEERS * GROUPS
CHUNK = GROUPS + 8
PIECE = 640
ALL = 64 * 1024 * 1024
LIMIT = 48_000_000
PROJECT_LIMIT = 53_500_000
FLOOR = -1e30
SCALE = 0.125
LOG_SCALE = 0.125 * math.log2(math.e)
BF = jnp.bfloat16
F32 = jnp.float32


def nn(a, b):
    return lax.dot_general(a, b, (((1,), (0,)), ((), ())), preferred_element_type=F32)


def nt(a, b):
    return lax.dot_general(a, b, (((1,), (1,)), ((), ())), preferred_element_type=F32)


def tn(a, b):
    return lax.dot_general(a, b, (((0,), (0,)), ((), ())), preferred_element_type=F32)


def iota(shape, dim):
    return lax.broadcasted_iota(jnp.int32, shape, dim)


def mark(mask):
    return jnp.where(mask, 1.0, 0.0).astype(BF)


def split3(x):
    high = x.astype(BF)
    rest = x - high.astype(F32)
    middle = rest.astype(BF)
    low = (rest - middle.astype(F32)).astype(BF)
    return high.astype(F32), middle.astype(F32), low.astype(F32)


def key_bias(count, live):
    return jnp.where(iota((1, count), 1) < live, 0.0, FLOOR)


def far_rows():
    r = iota((FAR, ROWS), 0)
    return mark(((r & (GROUPS - 1)) * STRIDE + (r >> 5)) == iota((FAR, ROWS), 1))


def own_head():
    return (iota((FAR, INNER), 0) >> 5) == (iota((FAR, INNER), 1) >> 6)


def fold(offset):
    return mark((iota((INNER, 128), 0) & (HD - 1)) + offset == iota((INNER, 128), 1))


def pack_kernel(pos_ref, tiles_ref, send_ref, slot_ref):
    places = pos_ref[...]
    block = places >> 9
    member = iota((PEERS, ROWS), 0) == block
    before = mark(iota((ROWS, ROWS), 0) < iota((ROWS, ROWS), 1))
    counts = nn(mark(member), before)
    rank = jnp.sum(jnp.where(member, counts, 0.0), 0, keepdims=True)
    slot = block * PORTION + rank.astype(jnp.int32)
    slot_ref[...] = slot
    order = mark(iota((ROWS, ROWS), 0) == slot)
    send_ref[:, :WIDTH] = nn(order, tiles_ref[...]).astype(BF)
    inside = places & (ROWS - 1)
    line = iota((128, ROWS), 0)
    code = jnp.where(line == 0, inside >> 4, jnp.where(line == 1, inside & 15, 0))
    send_ref[:, WIDTH:] = nt(order, code.astype(F32).astype(BF)).astype(BF)


def project_kernel(
    scal_ref, recv_ref, weight_ref, grad_ref, send_ref, q_ref, kv_ref, code_ref, far_ref, fgrad_ref, mean_ref
):
    lane = iota((8, 128), 1)
    pick = jnp.where(iota((8, 128), 0) == 0, jnp.where(lane == 0, 16.0, jnp.where(lane == 1, 1.0, 0.0)), 0.0)
    code = recv_ref[:, WIDTH:]
    code_ref[...] = code
    code_ref.send()
    place = nt(pick.astype(BF), code)[0:1].astype(jnp.int32)
    order = mark(iota((ROWS, ROWS), 0) == place)
    sequence = nn(order, recv_ref[:, :WIDTH]).astype(BF)
    proj = nn(sequence, weight_ref[...]).astype(BF)
    q_ref[...] = proj[:, :INNER]
    kv_ref[...] = proj[:, INNER:]
    q_ref.send()
    kv_ref.send()
    chosen = far_rows()
    own = own_head()
    far = nn(chosen, proj)
    fq = jnp.where(own, far[:, :INNER], 0.0).astype(BF)
    fk = jnp.where(own, far[:, INNER : 2 * INNER], 0.0).astype(BF)
    fv = jnp.where(own, far[:, 2 * INNER :], 0.0).astype(BF)
    fgrad = jnp.where(own, nn(chosen, grad_ref[...]), 0.0).astype(BF)
    far_ref[...] = fq
    fgrad_ref[...] = fgrad
    far_ref.send()
    fgrad_ref.send()
    scores = nt(fq, proj[:, INNER : 2 * INNER]) * LOG_SCALE + key_bias(ROWS, scal_ref[0])
    top = jnp.max(scores, -1, keepdims=True)
    weight = jnp.exp2(scores - top)
    total = jnp.sum(weight, -1, keepdims=True)
    mean = jnp.where(own, nn(weight.astype(BF), proj[:, 2 * INNER :]) / total, 0.0)
    mean_ref[:, :INNER] = mean
    lse = top + jnp.log2(total)
    mean_ref[:, INNER:] = jnp.broadcast_to(lse, (FAR, 128))
    mean_ref.send()
    inner = jnp.sum(fgrad.astype(F32) * mean, -1, keepdims=True)
    first, second = fold(0), fold(HD)
    key_value = (nn(fk, first) + nn(fv, second)).astype(BF)
    query_grad = (nn(fq, first) + nn(fgrad, second)).astype(BF)
    column = iota((FAR, 128), 1)
    stats = jnp.zeros((FAR, 128), F32)
    for at, part in enumerate(split3(lse) + split3(inner)):
        stats = jnp.where(column == at, part, stats)
    stats = jnp.concatenate([stats, jnp.zeros((QUERIES - FAR, 128), F32)], 0).astype(BF)
    stats = nt(mark(iota((8, 128), 0) == iota((8, 128), 1)), stats).astype(BF)
    for peer in range(PEERS):
        head = (peer % 8) % HEADS
        rows = slice(head * GROUPS, (head + 1) * GROUPS)
        send_ref[peer, :GROUPS, :128] = key_value[rows]
        send_ref[peer, :GROUPS, 128:] = query_grad[rows]
        send_ref[peer, GROUPS:, :] = stats


def local_kernel(scal_ref, q_ref, kv_ref, grad_ref, att_ref, dq_ref, dk_ref, dv_ref):
    live = scal_ref[0]
    bias = key_bias(ROWS, live)
    row = iota((ROWS, 128), 0)
    side = iota((ROWS, 128), 1) >> 6
    zero = jnp.zeros((), BF)
    for pair in range(HEADS // 2):
        lanes = slice(pair * 128, pair * 128 + 128)
        q = q_ref[:, lanes]
        k = kv_ref[:, lanes]
        v = kv_ref[:, INNER + pair * 128 : INNER + pair * 128 + 128]
        grad = grad_ref[:, lanes]
        atts, dqs, dks, dvs = [], [], [], []
        for half in range(2):
            ours = side == half
            kept = ours & ((row & (STRIDE - 1)) != pair * 2 + half)
            query = jnp.where(ours, q, zero)
            out_grad = jnp.where(kept, grad, zero)
            scores = nt(query, k) * LOG_SCALE + bias
            weight = jnp.exp2(scores - jnp.max(scores, -1, keepdims=True))
            inverse = 1.0 / jnp.sum(weight, -1, keepdims=True)
            result = jnp.where(kept & (row < live), nn(weight.astype(BF), v) * inverse, 0.0)
            stat = jnp.sum(out_grad.astype(F32) * result, -1, keepdims=True)
            prob = weight * inverse
            dscore = (prob * (nt(out_grad, v) - stat) * SCALE).astype(BF)
            atts.append(result)
            dqs.append(jnp.where(kept, nn(dscore, k), 0.0))
            dks.append(tn(dscore, query))
            dvs.append(tn(prob.astype(BF), out_grad))
        att_ref[:, lanes] = (atts[0] + atts[1]).astype(BF)
        dq_ref[:, lanes] = (dqs[0] + dqs[1]).astype(BF)
        dk_ref[:, lanes] = dks[0] + dks[1]
        dv_ref[:, lanes] = dvs[0] + dvs[1]


def far_kernel(scal_ref, recv_ref, tie_ref, send_ref, lse_ref, stat_ref, share_ref, num_ref):
    first = scal_ref[2] * 8
    head = scal_ref[3]
    left = iota((QUERIES, 128), 1) < HD
    zero = jnp.zeros((), BF)
    pick = mark(iota((GROUPS, QUERIES), 1) == iota((GROUPS, QUERIES), 0) + head * GROUPS)
    kv = recv_ref[:, :GROUPS, :128].reshape(KEYS, 128)
    own_kv = recv_ref[pl.ds(first, 8), :GROUPS, :128].reshape(QUERIES, 128)
    last = scal_ref[1] - head
    bias = jnp.where(iota((1, KEYS), 1) * STRIDE < last, 0.0, FLOOR)
    own_bias = jnp.where((iota((1, QUERIES), 1) + first * GROUPS) * STRIDE < last, 0.0, FLOOR)
    key_out = jnp.zeros((QUERIES, 128), F32)
    value_out = jnp.zeros((QUERIES, 128), F32)
    for i in range(4):
        rows = slice(i * QUERIES, (i + 1) * QUERIES)
        mine = recv_ref[8 * i : 8 * i + 8, :GROUPS, 128:].reshape(QUERIES, 128)
        query = jnp.where(left, mine, zero)
        grad = jnp.where(left, zero, mine)
        parts = jnp.concatenate([nt(pick, recv_ref[8 * i + j, GROUPS:, :]) for j in range(8)], 0)
        lse = parts[:, 0:1] + parts[:, 1:2] + parts[:, 2:3]
        inner = parts[:, 3:4] + parts[:, 4:5] + parts[:, 5:6]
        scores = nt(query, kv) * LOG_SCALE + bias
        top = jnp.max(scores, -1, keepdims=True)
        weight = jnp.exp2(scores - top)
        ceiling = jnp.maximum(top, lse)
        gain = jnp.exp2(top - ceiling)
        near = jnp.exp2(lse - ceiling)
        total = jnp.sum(weight, -1, keepdims=True) * gain + near
        inverse = 1.0 / total
        share = near * inverse
        numerator = nn(weight.astype(BF), kv) * (gain * inverse)
        stat = jnp.sum(grad.astype(F32) * numerator, -1, keepdims=True) + share * inner
        lse = ceiling + jnp.log2(total)
        prob = jnp.exp2(nt(query, own_kv) * LOG_SCALE + own_bias - lse)
        dscore = (prob * (nt(grad, own_kv) - stat) * SCALE).astype(BF)
        key_out = key_out + tn(dscore, mine)
        value_out = value_out + tn(prob.astype(BF), mine)
        lse_ref[rows] = jnp.broadcast_to(lse, (QUERIES, 128))
        stat_ref[rows] = jnp.broadcast_to(stat, (QUERIES, 128))
        share_ref[rows] = jnp.broadcast_to(share, (QUERIES, 128))
        num_ref[rows] = numerator
    rows = pl.ds(pl.multiple_of(scal_ref[2] * QUERIES, QUERIES), QUERIES)
    mine = recv_ref[pl.ds(first, 8), :GROUPS, 128:].reshape(QUERIES, 128)
    query = jnp.where(left, mine, zero)
    grad = jnp.where(left, zero, mine)
    prob = jnp.exp2(nt(query, kv) * LOG_SCALE + bias - lse_ref[rows, 0:1])
    dscore = (prob * (nt(grad, kv) - stat_ref[rows, 0:1]) * SCALE).astype(BF)
    query_out = jnp.where(left, nn(dscore, kv), num_ref[rows]).astype(BF)
    key_out = jnp.where(left, key_out, value_out).astype(BF)
    column = iota((QUERIES, 128), 1)
    stats = jnp.zeros((QUERIES, 128), F32)
    for at, part in enumerate(split3(share_ref[rows])):
        stats = jnp.where(column == at, part, stats)
    stats = nt(mark(iota((8, 128), 0) == iota((8, 128), 1)), stats.astype(BF)).astype(BF)
    for j in range(8):
        send_ref[j, :GROUPS, :128] = key_out[j * GROUPS : (j + 1) * GROUPS]
        send_ref[j, :GROUPS, 128:] = query_out[j * GROUPS : (j + 1) * GROUPS]
        send_ref[j, GROUPS:, :] = stats


def returned_far(scal_ref, recv_ref):
    pick = mark(iota((GROUPS, QUERIES), 1) == iota((GROUPS, QUERIES), 0) + scal_ref[4] * GROUPS)
    shares = jnp.concatenate([nt(pick, recv_ref[h, GROUPS:, :]) for h in range(HEADS)], 0)
    share = shares[:, 0:1] + shares[:, 1:2] + shares[:, 2:3]
    query_out = recv_ref[:HEADS, :GROUPS, 128:].reshape(FAR, 128)
    return share, query_out


def far_result(scal_ref, share, query_out, mean):
    r = iota((FAR, INNER), 0)
    live = (r & (GROUPS - 1)) * STRIDE + (r >> 5) < scal_ref[0]
    numerator = nt(query_out, fold(HD))
    return jnp.where(live & own_head(), numerator + share * mean, 0.0)


def weight_pieces(result, att_ref, cot_ref, send_ref):
    attention = att_ref[...] + tn(far_rows(), result.astype(BF)).astype(BF)
    new = iota((INNER, INNER), 1)
    old = 3 * (8 * (new & 15) + ((new >> 4) & 7)) + (new >> 7)
    attention = nn(attention, mark(iota((INNER, INNER), 0) == old)).astype(BF)
    terms = (tn(attention, cot_ref[...]) * (1.0 / 512.0)).astype(BF)
    one, two, three = terms[:128], terms[128:256], terms[256:]
    pieces = (
        one[:, :PIECE],
        jnp.concatenate([one[:, 512:], two[:, :384]], 1),
        jnp.concatenate([two[:, 384:], three[:, :256]], 1),
        three[:, 128:],
    )
    for r in range(4):
        for q in range(8):
            send_ref[4 * q + r, :, WIDTH:] = pieces[r][16 * q : 16 * q + 16]


def finish_kernel(
    scal_ref,
    recv_ref,
    mean_ref,
    att_ref,
    cot_ref,
    far_ref,
    fgrad_ref,
    kv_ref,
    dk_ref,
    dv_ref,
    dq_ref,
    weight_ref,
    code_ref,
    send_ref,
    pair_ref,
):
    share, query_out = returned_far(scal_ref, recv_ref)
    result = far_result(scal_ref, share, query_out, mean_ref[:, :INNER])
    weight_pieces(result, att_ref, cot_ref, send_ref)
    fq, fgrad = far_ref[...], fgrad_ref[...]
    keys, values = kv_ref[:, :INNER], kv_ref[:, INNER:]
    stat = jnp.sum(fgrad.astype(F32) * result, -1, keepdims=True)
    scores = nt(fq, keys) * LOG_SCALE + key_bias(ROWS, scal_ref[0])
    prob = jnp.exp2(scores - mean_ref[:, INNER : INNER + 1]) * share
    dscore = (prob * (nt(fgrad, values) - stat) * SCALE).astype(BF)
    own = own_head()
    chosen = far_rows()
    far_dq = jnp.where(own, nn(dscore, keys) + nt(query_out, fold(0)), 0.0).astype(BF)
    pairs = recv_ref[:HEADS, :GROUPS, :128].reshape(FAR, 128)
    scaled = pairs.astype(F32) * 32.0
    pair_ref[0] = scaled[:, :HD]
    pair_ref[1] = scaled[:, HD:]
    far_dk = jnp.where(own, nt(pairs, fold(0)), 0.0).astype(BF)
    far_dv = jnp.where(own, nt(pairs, fold(HD)), 0.0).astype(BF)
    grad_query = dq_ref[...] + tn(chosen, far_dq).astype(BF)
    grad_key = (dk_ref[...] + tn(dscore, fq) + tn(chosen, far_dk)).astype(BF)
    grad_value = (dv_ref[...] + tn(prob.astype(BF), fgrad) + tn(chosen, far_dv)).astype(BF)
    rows = nt(grad_query, weight_ref[:, :INNER])
    rows = rows + nt(grad_key, weight_ref[:, INNER : 2 * INNER])
    rows = rows + nt(grad_value, weight_ref[:, 2 * INNER :])
    code = code_ref[...].astype(F32)
    place = (code[:, 0:1] * 16.0 + code[:, 1:2]).astype(jnp.int32)
    order = mark(iota((ROWS, ROWS), 1) == place)
    back = nn(order, rows.astype(BF)).astype(BF)
    for peer in range(PEERS):
        send_ref[peer, :, :WIDTH] = back[PORTION * peer : PORTION * (peer + 1)]


def pieces_kernel(scal_ref, got_ref, out_ref):
    total = got_ref[0, :, WIDTH:].astype(F32)
    for peer in range(1, PEERS):
        total = total + got_ref[peer, :, WIDTH:].astype(F32)
    turned = jnp.concatenate([total[:, HD:], total[:, :HD]], 1)
    total = jnp.where(scal_ref[5] == 1, turned, total)
    for k in range(PIECE // 128):
        out_ref[:, k, :] = total[:, k * 128 : (k + 1) * 128]
    out_ref[:, PIECE // 128 :, :] = jnp.zeros((16, 8 - PIECE // 128, 128), F32)


def unpack_kernel(slot_ref, rows_ref, out_ref):
    order = mark(iota((ROWS, ROWS), 0) == slot_ref[...])
    out_ref[...] = tn(order, rows_ref[:, :, :WIDTH].reshape(ROWS, WIDTH)).astype(BF)


class Late:
    def __init__(self, source, buffer, semaphore):
        self.buffer = buffer
        self.copy = pltpu.make_async_copy(source, buffer, semaphore)
        self.copy.start()
        self.ready = False

    def wait(self):
        if not self.ready:
            self.copy.wait()
            self.ready = True

    def __getitem__(self, index):
        self.wait()
        return self.buffer[index]


class Early:
    def __init__(self, target, buffer, semaphore):
        self.buffer = buffer
        self.copy = pltpu.make_async_copy(buffer, target, semaphore)
        self.sent = False

    def __setitem__(self, index, value):
        self.buffer[index] = value

    def send(self):
        if not self.sent:
            self.copy.start()
            self.sent = True


HERE, LATE, TIE, SCALAR = "here", "late", "tie", "scalar"
SPACES = {
    HERE: pl.BlockSpec(memory_space=pltpu.VMEM),
    TIE: pl.BlockSpec(memory_space=pl.ANY),
    SCALAR: pl.BlockSpec(memory_space=pltpu.SMEM),
}
FAR_AWAY = pl.BlockSpec(memory_space=pltpu.HBM)
QUERY = (0, ROWS, 0, INNER)
KEY_VALUE = (0, ROWS, INNER, 2 * INNER)
CODE = (0, ROWS, 3 * INNER, 128)
FAR_QUERY = (ROWS, FAR, 0, INNER)
FAR_GRAD = (ROWS, FAR, INNER, INNER)
MEAN = (0, FAR, 0, INNER + 128)
ATTENTION = (0, ROWS, 0, INNER)
GRAD_QUERY = (0, ROWS, INNER, INNER)
GRAD_KEY = (0, ROWS, 0, INNER)
GRAD_VALUE = (0, ROWS, INNER, INNER)
LEFT = ((6656, 3 * INNER + 128), BF, (QUERY, KEY_VALUE, CODE, FAR_QUERY, FAR_GRAD))
MEANS = ((8320, INNER + 128), F32, (MEAN,))
GRADS16 = ((11136, 2 * INNER), BF, (ATTENTION, GRAD_QUERY))
GRADS32 = ((5632, 2 * INNER), F32, (GRAD_KEY, GRAD_VALUE))


def part(ref, window):
    if window == LATE:
        return ref
    return ref.at[pl.ds(window[0], window[1]), pl.ds(window[2], window[3])]


def call(body, name, flops, ins, outs, scratch=(), limit=LIMIT):
    staged = []
    for array, kind in ins:
        if kind not in SPACES:
            staged.append((array.shape if kind == LATE else (kind[1], kind[3]), array.dtype))
    for dims, dtype, kind in outs:
        if kind == LATE:
            staged.append((dims, dtype))
        elif kind not in SPACES:
            staged += [((w[1], w[3]), dtype) for w in kind]

    def kernel(*refs):
        refs = list(refs)
        operands = [refs.pop(0) for _ in ins]
        targets = [refs.pop(0) for _ in outs]
        buffers = [refs.pop(0) for _ in staged]
        semaphores = refs.pop(0) if staged else None
        at = 0
        for i, (_, kind) in enumerate(ins):
            if kind not in SPACES:
                operands[i] = Late(part(operands[i], kind), buffers[at], semaphores.at[at])
                at += 1
        results = []
        for target, (_, _, kind) in zip(targets, outs):
            if kind in SPACES:
                results.append(target)
                continue
            for w in (LATE,) if kind == LATE else kind:
                results.append(Early(part(target, w), buffers[at], semaphores.at[at]))
                at += 1
        body(*operands, *results, *refs)
        for operand in operands:
            if isinstance(operand, Late):
                operand.wait()
        for result in results:
            if isinstance(result, Early):
                result.send()
        for result in results:
            if isinstance(result, Early):
                result.copy.wait()

    return pl.pallas_call(
        kernel,
        out_shape=[jax.ShapeDtypeStruct(dims, dtype) for dims, dtype, _ in outs],
        in_specs=[SPACES.get(kind, FAR_AWAY) for _, kind in ins],
        out_specs=[SPACES.get(kind, FAR_AWAY) for _, _, kind in outs],
        scratch_shapes=[pltpu.VMEM(dims, dtype) for dims, dtype in staged]
        + ([pltpu.SemaphoreType.DMA((len(staged),))] if staged else [])
        + list(scratch),
        name=name,
        compiler_params=pltpu.CompilerParams(vmem_limit_bytes=limit),
        cost_estimate=pl.CostEstimate(flops=flops, bytes_accessed=4_000_000, transcendentals=0),
    )(*[a for a, _ in ins])


def exchange(rows, axis):
    return lax.all_to_all(rows, axis, split_axis=0, concat_axis=0, tiled=True)


def local(tiles, tile_pos, lengths, qkv_weight, out_weight, cotangent):
    device = lax.axis_index("ctx")
    length = lengths[0]
    live = length - device * ROWS
    scal = jnp.stack([live, length, device // 8, (device % 8) % HEADS, device % 8, device % 2]).astype(jnp.int32)
    cot = cotangent[0]

    sent, slot = call(
        pack_kernel,
        "pack",
        800_000_000,
        [(tile_pos, LATE), (tiles[0], LATE)],
        [((ROWS, 896), BF, LATE), ((1, ROWS), jnp.int32, LATE)],
        limit=ALL,
    )
    got = exchange(sent.reshape(PEERS, PORTION, 896), "ctx").reshape(ROWS, 896)

    grad_attn = jnp.einsum("qd,cd->qc", cot, out_weight, preferred_element_type=F32).astype(BF)
    alive = lax.broadcasted_iota(jnp.int32, (ROWS, 1), 0) < live
    grad_out = jnp.where(alive, grad_attn, jnp.zeros((), BF))

    far_sent, left, means = call(
        project_kernel,
        "project",
        3_000_000_000,
        [(scal, SCALAR), (got, HERE), (qkv_weight, LATE), (grad_out, LATE)],
        [((PEERS, CHUNK, 256), BF, LATE), LEFT, MEANS],
        limit=PROJECT_LIMIT,
    )
    far_got = exchange(far_sent, "ctx")

    grads16, grads32 = call(
        local_kernel,
        "local_rows",
        12_000_000_000,
        [(scal, SCALAR), (left, QUERY), (left, KEY_VALUE), (grad_out, LATE)],
        [GRADS16, GRADS32],
    )

    (far_back,) = call(
        far_kernel,
        "far",
        6_000_000_000,
        [(scal, SCALAR), (far_got, HERE), (grads16, TIE)],
        [((8, CHUNK, 256), BF, HERE)],
        [pltpu.VMEM((KEYS, 128), F32)] * 4,
    )
    blocks = [[8 * b + j for j in range(8)] for b in range(PEERS // 8)]
    far_back = lax.all_to_all(
        far_back, "ctx", split_axis=0, concat_axis=0, axis_index_groups=blocks, tiled=True
    )

    back, pair = call(
        finish_kernel,
        "finish",
        4_000_000_000,
        [
            (scal, SCALAR),
            (far_back, HERE),
            (means, MEAN),
            (grads16, ATTENTION),
            (cot, LATE),
            (left, FAR_QUERY),
            (left, FAR_GRAD),
            (left, KEY_VALUE),
            (grads32, GRAD_KEY),
            (grads32, GRAD_VALUE),
            (grads16, GRAD_QUERY),
            (qkv_weight, LATE),
            (left, CODE),
        ],
        [((PEERS, PORTION, WIDTH + PIECE), BF, HERE), ((2, FAR, HD), F32, LATE)],
    )
    returned = exchange(back, "ctx")
    (pieces,) = call(
        pieces_kernel,
        "pieces",
        1_000_000,
        [(scal, SCALAR), (returned, HERE)],
        [((16, 8, 128), F32, HERE)],
    )
    pieces = exchange(pieces, "slide")
    weight_grad = jnp.sum(pieces, 0).reshape(-1)[:576]
    (tile_grads,) = call(
        unpack_kernel, "unpack", 400_000_000, [(slot, LATE), (returned, HERE)], [((ROWS, WIDTH), BF, LATE)]
    )
    return (tile_grads[None], weight_grad, pair.reshape(1, 2, HEADS, GROUPS, HD))


def solution(mesh):
    placed = (
        P("slide", "ctx", None),
        P("slide", "ctx"),
        P("slide"),
        P(),
        P(),
        P("slide", "ctx", None),
    )
    return jax.shard_map(
        local,
        mesh=mesh,
        in_specs=placed,
        out_specs=(
            P("slide", "ctx", None),
            P(("slide", "ctx")),
            P("slide", None, None, "ctx", None),
        ),
        check_vma=False,
    )
```

```python
import math

import jax
import jax.numpy as jnp
from jax import lax
from jax.experimental import pallas as pl
from jax.experimental.pallas import tpu as pltpu
from jax.sharding import PartitionSpec as P

HD = 64
HEADS = 6
STRIDE = 16
PEERS = 32
ROWS = 512
PORTION = 16
GROUPS = ROWS // STRIDE
FAR = HEADS * GROUPS
WIDTH = 768
INNER = HEADS * HD
QUERIES = 8 * GROUPS
KEYS = PEERS * GROUPS
CHUNK = GROUPS + 8
PIECE = 640
ALL = 64 * 1024 * 1024
LIMIT = 48_000_000
PROJECT_LIMIT = 53_500_000
FLOOR = -1e30
SCALE = 0.125
LOG_SCALE = 0.125 * math.log2(math.e)
BF = jnp.bfloat16
F32 = jnp.float32


def nn(a, b):
    return lax.dot_general(a, b, (((1,), (0,)), ((), ())), preferred_element_type=F32)


def nt(a, b):
    return lax.dot_general(a, b, (((1,), (1,)), ((), ())), preferred_element_type=F32)


def tn(a, b):
    return lax.dot_general(a, b, (((0,), (0,)), ((), ())), preferred_element_type=F32)


def iota(shape, dim):
    return lax.broadcasted_iota(jnp.int32, shape, dim)


def mark(mask):
    return jnp.where(mask, 1.0, 0.0).astype(BF)


def split3(x):
    high = x.astype(BF)
    rest = x - high.astype(F32)
    middle = rest.astype(BF)
    low = (rest - middle.astype(F32)).astype(BF)
    return high.astype(F32), middle.astype(F32), low.astype(F32)


def key_bias(count, live):
    return jnp.where(iota((1, count), 1) < live, 0.0, FLOOR)


def far_rows():
    r = iota((FAR, ROWS), 0)
    return mark(((r & (GROUPS - 1)) * STRIDE + (r >> 5)) == iota((FAR, ROWS), 1))


def own_head():
    return (iota((FAR, INNER), 0) >> 5) == (iota((FAR, INNER), 1) >> 6)


def fold(offset):
    return mark((iota((INNER, 128), 0) & (HD - 1)) + offset == iota((INNER, 128), 1))


def pack_kernel(pos_ref, tiles_ref, send_ref, slot_ref):
    places = pos_ref[...]
    block = places >> 9
    member = iota((PEERS, ROWS), 0) == block
    before = mark(iota((ROWS, ROWS), 0) < iota((ROWS, ROWS), 1))
    counts = nn(mark(member), before)
    rank = jnp.sum(jnp.where(member, counts, 0.0), 0, keepdims=True)
    slot = block * PORTION + rank.astype(jnp.int32)
    slot_ref[...] = slot
    order = mark(iota((ROWS, ROWS), 0) == slot)
    send_ref[:, :WIDTH] = nn(order, tiles_ref[...]).astype(BF)
    inside = places & (ROWS - 1)
    line = iota((128, ROWS), 0)
    code = jnp.where(line == 0, inside >> 4, jnp.where(line == 1, inside & 15, 0))
    send_ref[:, WIDTH:] = nt(order, code.astype(F32).astype(BF)).astype(BF)


def grad_kernel(scal_ref, cot_ref, weight_ref, out_ref):
    grad = nt(cot_ref[...], weight_ref[...]).astype(BF)
    out_ref[...] = jnp.where(iota((ROWS, INNER), 0) < scal_ref[0], grad, jnp.zeros((), BF))


def project_kernel(
    scal_ref, recv_ref, weight_ref, grad_ref, send_ref, q_ref, kv_ref, code_ref, far_ref, fgrad_ref, mean_ref
):
    lane = iota((8, 128), 1)
    pick = jnp.where(iota((8, 128), 0) == 0, jnp.where(lane == 0, 16.0, jnp.where(lane == 1, 1.0, 0.0)), 0.0)
    code = recv_ref[:, WIDTH:]
    code_ref[...] = code
    code_ref.send()
    place = nt(pick.astype(BF), code)[0:1].astype(jnp.int32)
    order = mark(iota((ROWS, ROWS), 0) == place)
    sequence = nn(order, recv_ref[:, :WIDTH]).astype(BF)
    proj = nn(sequence, weight_ref[...]).astype(BF)
    q_ref[...] = proj[:, :INNER]
    kv_ref[...] = proj[:, INNER:]
    q_ref.send()
    kv_ref.send()
    chosen = far_rows()
    own = own_head()
    far = nn(chosen, proj)
    fq = jnp.where(own, far[:, :INNER], 0.0).astype(BF)
    fk = jnp.where(own, far[:, INNER : 2 * INNER], 0.0).astype(BF)
    fv = jnp.where(own, far[:, 2 * INNER :], 0.0).astype(BF)
    fgrad = jnp.where(own, nn(chosen, grad_ref[...]), 0.0).astype(BF)
    far_ref[...] = fq
    fgrad_ref[...] = fgrad
    far_ref.send()
    fgrad_ref.send()
    scores = nt(fq, proj[:, INNER : 2 * INNER]) * LOG_SCALE + key_bias(ROWS, scal_ref[0])
    top = jnp.max(scores, -1, keepdims=True)
    weight = jnp.exp2(scores - top)
    total = jnp.sum(weight, -1, keepdims=True)
    mean = jnp.where(own, nn(weight.astype(BF), proj[:, 2 * INNER :]) / total, 0.0)
    mean_ref[:, :INNER] = mean
    lse = top + jnp.log2(total)
    mean_ref[:, INNER:] = jnp.broadcast_to(lse, (FAR, 128))
    mean_ref.send()
    inner = jnp.sum(fgrad.astype(F32) * mean, -1, keepdims=True)
    first, second = fold(0), fold(HD)
    key_value = (nn(fk, first) + nn(fv, second)).astype(BF)
    query_grad = (nn(fq, first) + nn(fgrad, second)).astype(BF)
    column = iota((FAR, 128), 1)
    stats = jnp.zeros((FAR, 128), F32)
    for at, part in enumerate(split3(lse) + split3(inner)):
        stats = jnp.where(column == at, part, stats)
    stats = jnp.concatenate([stats, jnp.zeros((QUERIES - FAR, 128), F32)], 0).astype(BF)
    stats = nt(mark(iota((8, 128), 0) == iota((8, 128), 1)), stats).astype(BF)
    for peer in range(PEERS):
        head = (peer % 8) % HEADS
        rows = slice(head * GROUPS, (head + 1) * GROUPS)
        send_ref[peer, :GROUPS, :128] = key_value[rows]
        send_ref[peer, :GROUPS, 128:] = query_grad[rows]
        send_ref[peer, GROUPS:, :] = stats


def local_kernel(
    scal_ref,
    q_ref,
    kv_ref,
    grad_ref,
    code_ref,
    far_ref,
    fgrad_ref,
    mean_ref,
    kv_out,
    code_out,
    far_out,
    fgrad_out,
    mean_out,
    att_ref,
    dq_ref,
    dk_ref,
    dv_ref,
):
    for held, out in (
        (kv_ref, kv_out),
        (code_ref, code_out),
        (far_ref, far_out),
        (fgrad_ref, fgrad_out),
        (mean_ref, mean_out),
    ):
        out[...] = held[...]
        out.send()
    live = scal_ref[0]
    bias = key_bias(ROWS, live)
    row = iota((ROWS, 128), 0)
    side = iota((ROWS, 128), 1) >> 6
    zero = jnp.zeros((), BF)
    for pair in range(HEADS // 2):
        lanes = slice(pair * 128, pair * 128 + 128)
        q = q_ref[:, lanes]
        k = kv_ref[:, lanes]
        v = kv_ref[:, INNER + pair * 128 : INNER + pair * 128 + 128]
        grad = grad_ref[:, lanes]
        atts, dqs, dks, dvs = [], [], [], []
        for half in range(2):
            ours = side == half
            kept = ours & ((row & (STRIDE - 1)) != pair * 2 + half)
            query = jnp.where(ours, q, zero)
            out_grad = jnp.where(kept, grad, zero)
            scores = nt(query, k) * LOG_SCALE + bias
            weight = jnp.exp2(scores - jnp.max(scores, -1, keepdims=True))
            inverse = 1.0 / jnp.sum(weight, -1, keepdims=True)
            result = jnp.where(kept & (row < live), nn(weight.astype(BF), v) * inverse, 0.0)
            stat = jnp.sum(out_grad.astype(F32) * result, -1, keepdims=True)
            prob = weight * inverse
            dscore = (prob * (nt(out_grad, v) - stat) * SCALE).astype(BF)
            atts.append(result)
            dqs.append(jnp.where(kept, nn(dscore, k), 0.0))
            dks.append(tn(dscore, query))
            dvs.append(tn(prob.astype(BF), out_grad))
        att_ref[:, lanes] = (atts[0] + atts[1]).astype(BF)
        dq_ref[:, lanes] = (dqs[0] + dqs[1]).astype(BF)
        dk_ref[:, lanes] = dks[0] + dks[1]
        dv_ref[:, lanes] = dvs[0] + dvs[1]


def far_kernel(scal_ref, recv_ref, tie_ref, send_ref, lse_ref, stat_ref, share_ref, num_ref):
    first = scal_ref[2] * 8
    head = scal_ref[3]
    left = iota((QUERIES, 128), 1) < HD
    zero = jnp.zeros((), BF)
    pick = mark(iota((GROUPS, QUERIES), 1) == iota((GROUPS, QUERIES), 0) + head * GROUPS)
    kv = recv_ref[:, :GROUPS, :128].reshape(KEYS, 128)
    own_kv = recv_ref[pl.ds(first, 8), :GROUPS, :128].reshape(QUERIES, 128)
    last = scal_ref[1] - head
    bias = jnp.where(iota((1, KEYS), 1) * STRIDE < last, 0.0, FLOOR)
    own_bias = jnp.where((iota((1, QUERIES), 1) + first * GROUPS) * STRIDE < last, 0.0, FLOOR)
    key_out = jnp.zeros((QUERIES, 128), F32)
    value_out = jnp.zeros((QUERIES, 128), F32)
    for i in range(4):
        rows = slice(i * QUERIES, (i + 1) * QUERIES)
        mine = recv_ref[8 * i : 8 * i + 8, :GROUPS, 128:].reshape(QUERIES, 128)
        query = jnp.where(left, mine, zero)
        grad = jnp.where(left, zero, mine)
        parts = jnp.concatenate([nt(pick, recv_ref[8 * i + j, GROUPS:, :]) for j in range(8)], 0)
        lse = parts[:, 0:1] + parts[:, 1:2] + parts[:, 2:3]
        inner = parts[:, 3:4] + parts[:, 4:5] + parts[:, 5:6]
        scores = nt(query, kv) * LOG_SCALE + bias
        top = jnp.max(scores, -1, keepdims=True)
        weight = jnp.exp2(scores - top)
        ceiling = jnp.maximum(top, lse)
        gain = jnp.exp2(top - ceiling)
        near = jnp.exp2(lse - ceiling)
        total = jnp.sum(weight, -1, keepdims=True) * gain + near
        inverse = 1.0 / total
        share = near * inverse
        numerator = nn(weight.astype(BF), kv) * (gain * inverse)
        stat = jnp.sum(grad.astype(F32) * numerator, -1, keepdims=True) + share * inner
        lse = ceiling + jnp.log2(total)
        prob = jnp.exp2(nt(query, own_kv) * LOG_SCALE + own_bias - lse)
        dscore = (prob * (nt(grad, own_kv) - stat) * SCALE).astype(BF)
        key_out = key_out + tn(dscore, mine)
        value_out = value_out + tn(prob.astype(BF), mine)
        lse_ref[rows] = jnp.broadcast_to(lse, (QUERIES, 128))
        stat_ref[rows] = jnp.broadcast_to(stat, (QUERIES, 128))
        share_ref[rows] = jnp.broadcast_to(share, (QUERIES, 128))
        num_ref[rows] = numerator
    rows = pl.ds(pl.multiple_of(scal_ref[2] * QUERIES, QUERIES), QUERIES)
    mine = recv_ref[pl.ds(first, 8), :GROUPS, 128:].reshape(QUERIES, 128)
    query = jnp.where(left, mine, zero)
    grad = jnp.where(left, zero, mine)
    prob = jnp.exp2(nt(query, kv) * LOG_SCALE + bias - lse_ref[rows, 0:1])
    dscore = (prob * (nt(grad, kv) - stat_ref[rows, 0:1]) * SCALE).astype(BF)
    query_out = jnp.where(left, nn(dscore, kv), num_ref[rows]).astype(BF)
    key_out = jnp.where(left, key_out, value_out).astype(BF)
    column = iota((QUERIES, 128), 1)
    stats = jnp.zeros((QUERIES, 128), F32)
    for at, part in enumerate(split3(share_ref[rows])):
        stats = jnp.where(column == at, part, stats)
    stats = nt(mark(iota((8, 128), 0) == iota((8, 128), 1)), stats.astype(BF)).astype(BF)
    for j in range(8):
        send_ref[j, :GROUPS, :128] = key_out[j * GROUPS : (j + 1) * GROUPS]
        send_ref[j, :GROUPS, 128:] = query_out[j * GROUPS : (j + 1) * GROUPS]
        send_ref[j, GROUPS:, :] = stats


def returned_far(scal_ref, recv_ref):
    pick = mark(iota((GROUPS, QUERIES), 1) == iota((GROUPS, QUERIES), 0) + scal_ref[4] * GROUPS)
    shares = jnp.concatenate([nt(pick, recv_ref[h, GROUPS:, :]) for h in range(HEADS)], 0)
    share = shares[:, 0:1] + shares[:, 1:2] + shares[:, 2:3]
    query_out = recv_ref[:HEADS, :GROUPS, 128:].reshape(FAR, 128)
    return share, query_out


def far_result(scal_ref, share, query_out, mean):
    r = iota((FAR, INNER), 0)
    live = (r & (GROUPS - 1)) * STRIDE + (r >> 5) < scal_ref[0]
    numerator = nt(query_out, fold(HD))
    return jnp.where(live & own_head(), numerator + share * mean, 0.0)


def weight_pieces(result, att_ref, cot_ref, send_ref):
    attention = att_ref[...] + tn(far_rows(), result.astype(BF)).astype(BF)
    new = iota((INNER, INNER), 1)
    old = 3 * (8 * (new & 15) + ((new >> 4) & 7)) + (new >> 7)
    attention = nn(attention, mark(iota((INNER, INNER), 0) == old)).astype(BF)
    terms = (tn(attention, cot_ref[...]) * (1.0 / 512.0)).astype(BF)
    one, two, three = terms[:128], terms[128:256], terms[256:]
    pieces = (
        one[:, :PIECE],
        jnp.concatenate([one[:, 512:], two[:, :384]], 1),
        jnp.concatenate([two[:, 384:], three[:, :256]], 1),
        three[:, 128:],
    )
    for r in range(4):
        for q in range(8):
            send_ref[4 * q + r, :, WIDTH:] = pieces[r][16 * q : 16 * q + 16]


def finish_kernel(
    scal_ref,
    recv_ref,
    mean_ref,
    att_ref,
    cot_ref,
    far_ref,
    fgrad_ref,
    kv_ref,
    dk_ref,
    dv_ref,
    dq_ref,
    weight_ref,
    code_ref,
    send_ref,
    pair_ref,
):
    share, query_out = returned_far(scal_ref, recv_ref)
    result = far_result(scal_ref, share, query_out, mean_ref[:, :INNER])
    weight_pieces(result, att_ref, cot_ref, send_ref)
    fq, fgrad = far_ref[...], fgrad_ref[...]
    keys, values = kv_ref[:, :INNER], kv_ref[:, INNER:]
    stat = jnp.sum(fgrad.astype(F32) * result, -1, keepdims=True)
    scores = nt(fq, keys) * LOG_SCALE + key_bias(ROWS, scal_ref[0])
    prob = jnp.exp2(scores - mean_ref[:, INNER : INNER + 1]) * share
    dscore = (prob * (nt(fgrad, values) - stat) * SCALE).astype(BF)
    own = own_head()
    chosen = far_rows()
    far_dq = jnp.where(own, nn(dscore, keys) + nt(query_out, fold(0)), 0.0).astype(BF)
    pairs = recv_ref[:HEADS, :GROUPS, :128].reshape(FAR, 128)
    scaled = pairs.astype(F32) * 32.0
    pair_ref[0] = scaled[:, :HD]
    pair_ref[1] = scaled[:, HD:]
    far_dk = jnp.where(own, nt(pairs, fold(0)), 0.0).astype(BF)
    far_dv = jnp.where(own, nt(pairs, fold(HD)), 0.0).astype(BF)
    grad_query = dq_ref[...] + tn(chosen, far_dq).astype(BF)
    grad_key = (dk_ref[...] + tn(dscore, fq) + tn(chosen, far_dk)).astype(BF)
    grad_value = (dv_ref[...] + tn(prob.astype(BF), fgrad) + tn(chosen, far_dv)).astype(BF)
    rows = nt(grad_query, weight_ref[:, :INNER])
    rows = rows + nt(grad_key, weight_ref[:, INNER : 2 * INNER])
    rows = rows + nt(grad_value, weight_ref[:, 2 * INNER :])
    code = code_ref[...].astype(F32)
    place = (code[:, 0:1] * 16.0 + code[:, 1:2]).astype(jnp.int32)
    order = mark(iota((ROWS, ROWS), 1) == place)
    back = nn(order, rows.astype(BF)).astype(BF)
    for peer in range(PEERS):
        send_ref[peer, :, :WIDTH] = back[PORTION * peer : PORTION * (peer + 1)]


def pieces_kernel(scal_ref, got_ref, out_ref):
    total = got_ref[0, :, WIDTH:].astype(F32)
    for peer in range(1, PEERS):
        total = total + got_ref[peer, :, WIDTH:].astype(F32)
    turned = jnp.concatenate([total[:, HD:], total[:, :HD]], 1)
    total = jnp.where(scal_ref[5] == 1, turned, total)
    for k in range(PIECE // 128):
        out_ref[:, k, :] = total[:, k * 128 : (k + 1) * 128]
    out_ref[:, PIECE // 128 :, :] = jnp.zeros((16, 8 - PIECE // 128, 128), F32)


def unpack_kernel(slot_ref, rows_ref, out_ref):
    order = mark(iota((ROWS, ROWS), 0) == slot_ref[...])
    out_ref[...] = tn(order, rows_ref[:, :, :WIDTH].reshape(ROWS, WIDTH)).astype(BF)


class Late:
    def __init__(self, source, buffer, semaphore):
        self.buffer = buffer
        self.copy = pltpu.make_async_copy(source, buffer, semaphore)
        self.copy.start()
        self.ready = False

    def wait(self):
        if not self.ready:
            self.copy.wait()
            self.ready = True

    def __getitem__(self, index):
        self.wait()
        return self.buffer[index]


class Early:
    def __init__(self, target, buffer, semaphore):
        self.buffer = buffer
        self.copy = pltpu.make_async_copy(buffer, target, semaphore)
        self.sent = False

    def __setitem__(self, index, value):
        self.buffer[index] = value

    def send(self):
        if not self.sent:
            self.copy.start()
            self.sent = True


HERE, LATE, TIE, SCALAR = "here", "late", "tie", "scalar"
SPACES = {
    HERE: pl.BlockSpec(memory_space=pltpu.VMEM),
    TIE: pl.BlockSpec(memory_space=pl.ANY),
    SCALAR: pl.BlockSpec(memory_space=pltpu.SMEM),
}
FAR_AWAY = pl.BlockSpec(memory_space=pltpu.HBM)
QUERY = (0, ROWS, 0, INNER)
KEY_VALUE = (0, ROWS, INNER, 2 * INNER)
CODE = (0, ROWS, 3 * INNER, 128)
FAR_QUERY = (ROWS, FAR, 0, INNER)
FAR_GRAD = (ROWS, FAR, INNER, INNER)
MEAN = (0, FAR, 0, INNER + 128)
LEFT = ((6656, 3 * INNER + 128), BF, (QUERY, KEY_VALUE, CODE, FAR_QUERY, FAR_GRAD))
GRADS = ((21504, INNER), BF, (QUERY,))
MEANS = ((8320, INNER + 128), F32, (MEAN,))


def part(ref, window):
    if window == LATE:
        return ref
    return ref.at[pl.ds(window[0], window[1]), pl.ds(window[2], window[3])]


def scalars(lengths_ref):
    device = lax.axis_index("ctx")
    inner = device & 7
    length = lengths_ref[0]
    head = jnp.where(inner >= HEADS, inner - HEADS, inner)
    return (length - device * ROWS, length, device >> 3, head, inner, device & 1)


def call(body, name, flops, ins, outs, scratch=(), limit=LIMIT):
    staged = []
    for array, kind in ins:
        if kind not in SPACES:
            staged.append((array.shape if kind == LATE else (kind[1], kind[3]), array.dtype))
    for dims, dtype, kind in outs:
        if kind == LATE:
            staged.append((dims, dtype))
        elif kind not in SPACES:
            staged += [((w[1], w[3]), dtype) for w in kind]

    def kernel(*refs):
        refs = list(refs)
        operands = [refs.pop(0) for _ in ins]
        targets = [refs.pop(0) for _ in outs]
        buffers = [refs.pop(0) for _ in staged]
        semaphores = refs.pop(0) if staged else None
        at = 0
        for i, (_, kind) in enumerate(ins):
            if kind == SCALAR:
                operands[i] = scalars(operands[i])
            if kind not in SPACES:
                operands[i] = Late(part(operands[i], kind), buffers[at], semaphores.at[at])
                at += 1
        results = []
        for target, (_, _, kind) in zip(targets, outs):
            if kind in SPACES:
                results.append(target)
                continue
            for w in (LATE,) if kind == LATE else kind:
                results.append(Early(part(target, w), buffers[at], semaphores.at[at]))
                at += 1
        body(*operands, *results, *refs)
        for operand in operands:
            if isinstance(operand, Late):
                operand.wait()
        for result in results:
            if isinstance(result, Early):
                result.send()
        for result in results:
            if isinstance(result, Early):
                result.copy.wait()

    return pl.pallas_call(
        kernel,
        out_shape=[jax.ShapeDtypeStruct(dims, dtype) for dims, dtype, _ in outs],
        in_specs=[SPACES.get(kind, FAR_AWAY) for _, kind in ins],
        out_specs=[SPACES.get(kind, FAR_AWAY) for _, _, kind in outs],
        scratch_shapes=[pltpu.VMEM(dims, dtype) for dims, dtype in staged]
        + ([pltpu.SemaphoreType.DMA((len(staged),))] if staged else [])
        + list(scratch),
        name=name,
        compiler_params=pltpu.CompilerParams(vmem_limit_bytes=limit),
        cost_estimate=pl.CostEstimate(flops=flops, bytes_accessed=4_000_000, transcendentals=0),
    )(*[a for a, _ in ins])


def exchange(rows, axis):
    return lax.all_to_all(rows, axis, split_axis=0, concat_axis=0, tiled=True)


def local(tiles, tile_pos, lengths, qkv_weight, out_weight, cotangent):
    cot = cotangent[0]

    sent, slot = call(
        pack_kernel,
        "pack",
        800_000_000,
        [(tile_pos, LATE), (tiles[0], LATE)],
        [((ROWS, 896), BF, LATE), ((1, ROWS), jnp.int32, LATE)],
        limit=ALL,
    )
    got = exchange(sent.reshape(PEERS, PORTION, 896), "ctx").reshape(ROWS, 896)

    (grad_out,) = call(
        grad_kernel,
        "grad",
        400_000_000,
        [(lengths, SCALAR), (cot, LATE), (out_weight, LATE)],
        [GRADS],
    )

    far_sent, left, means = call(
        project_kernel,
        "project",
        3_000_000_000,
        [(lengths, SCALAR), (got, HERE), (qkv_weight, LATE), (grad_out, QUERY)],
        [((PEERS, CHUNK, 256), BF, LATE), LEFT, MEANS],
        limit=PROJECT_LIMIT,
    )
    far_got = exchange(far_sent, "ctx")

    key_value, code, far_q, far_grad, mean, att, dq, dk, dv, after = call(
        local_kernel,
        "local_rows",
        12_000_000_000,
        [
            (lengths, SCALAR),
            (left, QUERY),
            (left, KEY_VALUE),
            (grad_out, QUERY),
            (left, CODE),
            (left, FAR_QUERY),
            (left, FAR_GRAD),
            (means, MEAN),
        ],
        [
            ((ROWS, 2 * INNER), BF, LATE),
            ((ROWS, 128), BF, LATE),
            ((FAR, INNER), BF, LATE),
            ((FAR, INNER), BF, LATE),
            ((FAR, INNER + 128), F32, LATE),
            ((ROWS, INNER), BF, LATE),
            ((ROWS, INNER), BF, LATE),
            ((ROWS, INNER), F32, LATE),
            ((ROWS, INNER), F32, LATE),
            ((8320, 512), F32, ()),
        ],
        limit=ALL,
    )

    (far_back,) = call(
        far_kernel,
        "far",
        6_000_000_000,
        [(lengths, SCALAR), (far_got, HERE), (after, TIE)],
        [((8, CHUNK, 256), BF, HERE)],
        [pltpu.VMEM((KEYS, 128), F32)] * 4,
    )
    blocks = [[8 * b + j for j in range(8)] for b in range(PEERS // 8)]
    far_back = lax.all_to_all(
        far_back, "ctx", split_axis=0, concat_axis=0, axis_index_groups=blocks, tiled=True
    )

    back, pair = call(
        finish_kernel,
        "finish",
        4_000_000_000,
        [
            (lengths, SCALAR),
            (far_back, HERE),
            (mean, HERE),
            (att, HERE),
            (cot, HERE),
            (far_q, HERE),
            (far_grad, HERE),
            (key_value, HERE),
            (dk, HERE),
            (dv, HERE),
            (dq, HERE),
            (qkv_weight, HERE),
            (code, HERE),
        ],
        [((PEERS, PORTION, WIDTH + PIECE), BF, HERE), ((2, FAR, HD), F32, LATE)],
    )
    returned = exchange(back, "ctx")
    (pieces,) = call(
        pieces_kernel,
        "pieces",
        1_000_000,
        [(lengths, SCALAR), (returned, HERE)],
        [((16, 8, 128), F32, HERE)],
    )
    pieces = exchange(pieces, "slide")
    weight_grad = jnp.sum(pieces, 0).reshape(-1)[:576]
    (tile_grads,) = call(
        unpack_kernel, "unpack", 400_000_000, [(slot, LATE), (returned, HERE)], [((ROWS, WIDTH), BF, LATE)]
    )
    return (tile_grads[None], weight_grad, pair.reshape(1, 2, HEADS, GROUPS, HD))


def solution(mesh):
    placed = (
        P("slide", "ctx", None),
        P("slide", "ctx"),
        P("slide"),
        P(),
        P(),
        P("slide", "ctx", None),
    )
    return jax.shard_map(
        local,
        mesh=mesh,
        in_specs=placed,
        out_specs=(
            P("slide", "ctx", None),
            P(("slide", "ctx")),
            P("slide", None, None, "ctx", None),
        ),
        check_vma=False,
    )
```

```python
import math

import jax
import jax.numpy as jnp
from jax import lax
from jax.experimental import pallas as pl
from jax.experimental.pallas import tpu as pltpu
from jax.sharding import PartitionSpec as P

HD = 64
HEADS = 6
STRIDE = 16
PEERS = 32
ROWS = 512
PORTION = 16
GROUPS = ROWS // STRIDE
FAR = HEADS * GROUPS
WIDTH = 768
INNER = HEADS * HD
QUERIES = 8 * GROUPS
KEYS = PEERS * GROUPS
CHUNK = GROUPS + 8
PIECE = 640
ALL = 64 * 1024 * 1024
LIMIT = 42_000_000
PROJECT_LIMIT = 53_500_000
LOCAL_LIMIT = 54_400_000
FLOOR = -1e30
SCALE = 0.125
LOG_SCALE = 0.125 * math.log2(math.e)
BF = jnp.bfloat16
F32 = jnp.float32


def nn(a, b):
    return lax.dot_general(a, b, (((1,), (0,)), ((), ())), preferred_element_type=F32)


def nt(a, b):
    return lax.dot_general(a, b, (((1,), (1,)), ((), ())), preferred_element_type=F32)


def tn(a, b):
    return lax.dot_general(a, b, (((0,), (0,)), ((), ())), preferred_element_type=F32)


def iota(shape, dim):
    return lax.broadcasted_iota(jnp.int32, shape, dim)


def mark(mask):
    return jnp.where(mask, 1.0, 0.0).astype(BF)


def split3(x):
    high = x.astype(BF)
    rest = x - high.astype(F32)
    middle = rest.astype(BF)
    low = (rest - middle.astype(F32)).astype(BF)
    return high.astype(F32), middle.astype(F32), low.astype(F32)


def key_bias(count, live):
    return jnp.where(iota((1, count), 1) < live, 0.0, FLOOR)


def far_rows():
    r = iota((FAR, ROWS), 0)
    return mark(((r & (GROUPS - 1)) * STRIDE + (r >> 5)) == iota((FAR, ROWS), 1))


def own_head():
    return (iota((FAR, INNER), 0) >> 5) == (iota((FAR, INNER), 1) >> 6)


def fold(offset):
    return mark((iota((INNER, 128), 0) & (HD - 1)) + offset == iota((INNER, 128), 1))


def pack_kernel(pos_ref, tiles_ref, send_ref, slot_ref):
    places = pos_ref[...]
    block = places >> 9
    member = iota((PEERS, ROWS), 0) == block
    before = mark(iota((ROWS, ROWS), 0) < iota((ROWS, ROWS), 1))
    counts = nn(mark(member), before)
    rank = jnp.sum(jnp.where(member, counts, 0.0), 0, keepdims=True)
    slot = block * PORTION + rank.astype(jnp.int32)
    slot_ref[...] = slot
    order = mark(iota((ROWS, ROWS), 0) == slot)
    send_ref[:, :WIDTH] = nn(order, tiles_ref[...]).astype(BF)
    inside = places & (ROWS - 1)
    line = iota((128, ROWS), 0)
    code = jnp.where(line == 0, inside >> 4, jnp.where(line == 1, inside & 15, 0))
    send_ref[:, WIDTH:] = nt(order, code.astype(F32).astype(BF)).astype(BF)


def grad_kernel(scal_ref, cot_ref, weight_ref, out_ref):
    grad = nt(cot_ref[...], weight_ref[...]).astype(BF)
    out_ref[...] = jnp.where(iota((ROWS, INNER), 0) < scal_ref[0], grad, jnp.zeros((), BF))


def project_kernel(
    scal_ref, recv_ref, weight_ref, grad_ref, send_ref, q_ref, kv_ref, code_ref, far_ref, fgrad_ref, mean_ref
):
    lane = iota((8, 128), 1)
    pick = jnp.where(iota((8, 128), 0) == 0, jnp.where(lane == 0, 16.0, jnp.where(lane == 1, 1.0, 0.0)), 0.0)
    code = recv_ref[:, WIDTH:]
    code_ref[...] = code
    code_ref.send()
    place = nt(pick.astype(BF), code)[0:1].astype(jnp.int32)
    order = mark(iota((ROWS, ROWS), 0) == place)
    sequence = nn(order, recv_ref[:, :WIDTH]).astype(BF)
    proj = nn(sequence, weight_ref[...]).astype(BF)
    q_ref[...] = proj[:, :INNER]
    kv_ref[...] = proj[:, INNER:]
    q_ref.send()
    kv_ref.send()
    chosen = far_rows()
    own = own_head()
    far = nn(chosen, proj)
    fq = jnp.where(own, far[:, :INNER], 0.0).astype(BF)
    fk = jnp.where(own, far[:, INNER : 2 * INNER], 0.0).astype(BF)
    fv = jnp.where(own, far[:, 2 * INNER :], 0.0).astype(BF)
    fgrad = jnp.where(own, nn(chosen, grad_ref[...]), 0.0).astype(BF)
    far_ref[...] = fq
    fgrad_ref[...] = fgrad
    far_ref.send()
    fgrad_ref.send()
    scores = nt(fq, proj[:, INNER : 2 * INNER]) * LOG_SCALE + key_bias(ROWS, scal_ref[0])
    top = jnp.max(scores, -1, keepdims=True)
    weight = jnp.exp2(scores - top)
    total = jnp.sum(weight, -1, keepdims=True)
    mean = jnp.where(own, nn(weight.astype(BF), proj[:, 2 * INNER :]) / total, 0.0)
    mean_ref[:, :INNER] = mean
    lse = top + jnp.log2(total)
    mean_ref[:, INNER:] = jnp.broadcast_to(lse, (FAR, 128))
    mean_ref.send()
    inner = jnp.sum(fgrad.astype(F32) * mean, -1, keepdims=True)
    first, second = fold(0), fold(HD)
    key_value = (nn(fk, first) + nn(fv, second)).astype(BF)
    query_grad = (nn(fq, first) + nn(fgrad, second)).astype(BF)
    column = iota((FAR, 128), 1)
    stats = jnp.zeros((FAR, 128), F32)
    for at, part in enumerate(split3(lse) + split3(inner)):
        stats = jnp.where(column == at, part, stats)
    stats = jnp.concatenate([stats, jnp.zeros((QUERIES - FAR, 128), F32)], 0).astype(BF)
    stats = nt(mark(iota((8, 128), 0) == iota((8, 128), 1)), stats).astype(BF)
    for peer in range(PEERS):
        head = (peer % 8) % HEADS
        rows = slice(head * GROUPS, (head + 1) * GROUPS)
        send_ref[peer, :GROUPS, :128] = key_value[rows]
        send_ref[peer, :GROUPS, 128:] = query_grad[rows]
        send_ref[peer, GROUPS:, :] = stats


def local_kernel(
    scal_ref,
    q_ref,
    kv_ref,
    grad_ref,
    code_ref,
    far_ref,
    fgrad_ref,
    mean_ref,
    kv_out,
    code_out,
    far_out,
    fgrad_out,
    att_ref,
    dq_ref,
    mean_out,
    dk_ref,
    dv_ref,
):
    for held, out in (
        (kv_ref, kv_out),
        (code_ref, code_out),
        (far_ref, far_out),
        (fgrad_ref, fgrad_out),
        (mean_ref, mean_out),
    ):
        out[...] = held[...]
        out.send()
    live = scal_ref[0]
    bias = key_bias(ROWS, live)
    row = iota((ROWS, 128), 0)
    side = iota((ROWS, 128), 1) >> 6
    zero = jnp.zeros((), BF)
    for pair in range(HEADS // 2):
        lanes = slice(pair * 128, pair * 128 + 128)
        q = q_ref[:, lanes]
        k = kv_ref[:, lanes]
        v = kv_ref[:, INNER + pair * 128 : INNER + pair * 128 + 128]
        grad = grad_ref[:, lanes]
        atts, dqs, dks, dvs = [], [], [], []
        for half in range(2):
            ours = side == half
            kept = ours & ((row & (STRIDE - 1)) != pair * 2 + half)
            query = jnp.where(ours, q, zero)
            out_grad = jnp.where(kept, grad, zero)
            scores = nt(query, k) * LOG_SCALE + bias
            weight = jnp.exp2(scores - jnp.max(scores, -1, keepdims=True))
            inverse = 1.0 / jnp.sum(weight, -1, keepdims=True)
            result = jnp.where(kept & (row < live), nn(weight.astype(BF), v) * inverse, 0.0)
            stat = jnp.sum(out_grad.astype(F32) * result, -1, keepdims=True)
            prob = weight * inverse
            dscore = (prob * (nt(out_grad, v) - stat) * SCALE).astype(BF)
            atts.append(result)
            dqs.append(jnp.where(kept, nn(dscore, k), 0.0))
            dks.append(tn(dscore, query))
            dvs.append(tn(prob.astype(BF), out_grad))
        att_ref[:, lanes] = (atts[0] + atts[1]).astype(BF)
        dq_ref[:, lanes] = (dqs[0] + dqs[1]).astype(BF)
        dk_ref[:, lanes] = dks[0] + dks[1]
        dv_ref[:, lanes] = dvs[0] + dvs[1]


def far_kernel(scal_ref, recv_ref, tie_ref, send_ref, lse_ref, stat_ref, share_ref, num_ref):
    first = scal_ref[2] * 8
    head = scal_ref[3]
    left = iota((QUERIES, 128), 1) < HD
    zero = jnp.zeros((), BF)
    pick = mark(iota((GROUPS, QUERIES), 1) == iota((GROUPS, QUERIES), 0) + head * GROUPS)
    kv = recv_ref[:, :GROUPS, :128].reshape(KEYS, 128)
    own_kv = recv_ref[pl.ds(first, 8), :GROUPS, :128].reshape(QUERIES, 128)
    last = scal_ref[1] - head
    bias = jnp.where(iota((1, KEYS), 1) * STRIDE < last, 0.0, FLOOR)
    own_bias = jnp.where((iota((1, QUERIES), 1) + first * GROUPS) * STRIDE < last, 0.0, FLOOR)
    key_out = jnp.zeros((QUERIES, 128), F32)
    value_out = jnp.zeros((QUERIES, 128), F32)
    def asked(i):
        mine = recv_ref[8 * i : 8 * i + 8, :GROUPS, 128:].reshape(QUERIES, 128)
        query = jnp.where(left, mine, zero)
        grad = jnp.where(left, zero, mine)
        parts = jnp.concatenate([nt(pick, recv_ref[8 * i + j, GROUPS:, :]) for j in range(8)], 0)
        scores = nt(query, kv) * LOG_SCALE + bias
        own_scores = nt(query, own_kv) * LOG_SCALE + own_bias
        return mine, grad, parts, scores, own_scores, nt(grad, own_kv)

    following = asked(0)
    for i in range(4):
        rows = slice(i * QUERIES, (i + 1) * QUERIES)
        mine, grad, parts, scores, own_scores, own_dprob = following
        if i < 3:
            following = asked(i + 1)
        lse = parts[:, 0:1] + parts[:, 1:2] + parts[:, 2:3]
        inner = parts[:, 3:4] + parts[:, 4:5] + parts[:, 5:6]
        top = jnp.max(scores, -1, keepdims=True)
        weight = jnp.exp2(scores - top)
        ceiling = jnp.maximum(top, lse)
        gain = jnp.exp2(top - ceiling)
        near = jnp.exp2(lse - ceiling)
        total = jnp.sum(weight, -1, keepdims=True) * gain + near
        inverse = 1.0 / total
        share = near * inverse
        numerator = nn(weight.astype(BF), kv) * (gain * inverse)
        stat = jnp.sum(grad.astype(F32) * numerator, -1, keepdims=True) + share * inner
        lse = ceiling + jnp.log2(total)
        prob = jnp.exp2(own_scores - lse)
        dscore = (prob * (own_dprob - stat) * SCALE).astype(BF)
        key_out = key_out + tn(dscore, mine)
        value_out = value_out + tn(prob.astype(BF), mine)
        lse_ref[rows] = jnp.broadcast_to(lse, (QUERIES, 128))
        stat_ref[rows] = jnp.broadcast_to(stat, (QUERIES, 128))
        share_ref[rows] = jnp.broadcast_to(share, (QUERIES, 128))
        num_ref[rows] = numerator
    rows = pl.ds(pl.multiple_of(scal_ref[2] * QUERIES, QUERIES), QUERIES)
    mine = recv_ref[pl.ds(first, 8), :GROUPS, 128:].reshape(QUERIES, 128)
    query = jnp.where(left, mine, zero)
    grad = jnp.where(left, zero, mine)
    prob = jnp.exp2(nt(query, kv) * LOG_SCALE + bias - lse_ref[rows, 0:1])
    dscore = (prob * (nt(grad, kv) - stat_ref[rows, 0:1]) * SCALE).astype(BF)
    query_out = jnp.where(left, nn(dscore, kv), num_ref[rows]).astype(BF)
    key_out = jnp.where(left, key_out, value_out).astype(BF)
    column = iota((QUERIES, 128), 1)
    stats = jnp.zeros((QUERIES, 128), F32)
    for at, part in enumerate(split3(share_ref[rows])):
        stats = jnp.where(column == at, part, stats)
    stats = nt(mark(iota((8, 128), 0) == iota((8, 128), 1)), stats.astype(BF)).astype(BF)
    for j in range(8):
        send_ref[j, :GROUPS, :128] = key_out[j * GROUPS : (j + 1) * GROUPS]
        send_ref[j, :GROUPS, 128:] = query_out[j * GROUPS : (j + 1) * GROUPS]
        send_ref[j, GROUPS:, :] = stats


def returned_far(scal_ref, recv_ref):
    pick = mark(iota((GROUPS, QUERIES), 1) == iota((GROUPS, QUERIES), 0) + scal_ref[4] * GROUPS)
    shares = jnp.concatenate([nt(pick, recv_ref[h, GROUPS:, :]) for h in range(HEADS)], 0)
    share = shares[:, 0:1] + shares[:, 1:2] + shares[:, 2:3]
    query_out = recv_ref[:HEADS, :GROUPS, 128:].reshape(FAR, 128)
    return share, query_out


def far_result(scal_ref, share, query_out, mean):
    r = iota((FAR, INNER), 0)
    live = (r & (GROUPS - 1)) * STRIDE + (r >> 5) < scal_ref[0]
    numerator = nt(query_out, fold(HD))
    return jnp.where(live & own_head(), numerator + share * mean, 0.0)


def weight_pieces(result, att_ref, cot_ref, send_ref):
    attention = att_ref[...] + tn(far_rows(), result.astype(BF)).astype(BF)
    new = iota((INNER, INNER), 1)
    old = 3 * (8 * (new & 15) + ((new >> 4) & 7)) + (new >> 7)
    attention = nn(attention, mark(iota((INNER, INNER), 0) == old)).astype(BF)
    terms = (tn(attention, cot_ref[...]) * (1.0 / 512.0)).astype(BF)
    one, two, three = terms[:128], terms[128:256], terms[256:]
    pieces = (
        one[:, :PIECE],
        jnp.concatenate([one[:, 512:], two[:, :384]], 1),
        jnp.concatenate([two[:, 384:], three[:, :256]], 1),
        three[:, 128:],
    )
    for r in range(4):
        for q in range(8):
            send_ref[4 * q + r, :, WIDTH:] = pieces[r][16 * q : 16 * q + 16]


def finish_kernel(scal_ref, recv_ref, held16_ref, held32_ref, cot_ref, weight_ref, send_ref, pair_ref):
    kv_ref, code_ref, far_ref, fgrad_ref, att_ref, dq_ref = (part(held16_ref, w) for w in HELD16[2])
    mean_ref, dk_ref, dv_ref = (part(held32_ref, w) for w in HELD32[2])
    share, query_out = returned_far(scal_ref, recv_ref)
    result = far_result(scal_ref, share, query_out, mean_ref[:, :INNER])
    fq, fgrad = far_ref[...], fgrad_ref[...]
    keys, values = kv_ref[:, :INNER], kv_ref[:, INNER:]
    stat = jnp.sum(fgrad.astype(F32) * result, -1, keepdims=True)
    scores = nt(fq, keys) * LOG_SCALE + key_bias(ROWS, scal_ref[0])
    prob = jnp.exp2(scores - mean_ref[:, INNER : INNER + 1]) * share
    dscore = (prob * (nt(fgrad, values) - stat) * SCALE).astype(BF)
    own = own_head()
    chosen = far_rows()
    far_dq = jnp.where(own, nn(dscore, keys) + nt(query_out, fold(0)), 0.0).astype(BF)
    pairs = recv_ref[:HEADS, :GROUPS, :128].reshape(FAR, 128)
    scaled = pairs.astype(F32) * 32.0
    pair_ref[0] = scaled[:, :HD]
    pair_ref[1] = scaled[:, HD:]
    far_dk = jnp.where(own, nt(pairs, fold(0)), 0.0).astype(BF)
    far_dv = jnp.where(own, nt(pairs, fold(HD)), 0.0).astype(BF)
    grad_query = dq_ref[...] + tn(chosen, far_dq).astype(BF)
    grad_key = (dk_ref[...] + tn(jnp.concatenate([dscore, chosen], 0), jnp.concatenate([fq, far_dk], 0))).astype(BF)
    both = jnp.concatenate([prob.astype(BF), chosen], 0)
    grad_value = (dv_ref[...] + tn(both, jnp.concatenate([fgrad, far_dv], 0))).astype(BF)
    weight_pieces(result, att_ref, cot_ref, send_ref)
    rows = nt(jnp.concatenate([grad_query, grad_key, grad_value], 1), weight_ref[...])
    code = code_ref[...].astype(F32)
    place = (code[:, 0:1] * 16.0 + code[:, 1:2]).astype(jnp.int32)
    order = mark(iota((ROWS, ROWS), 1) == place)
    back = nn(order, rows.astype(BF)).astype(BF)
    for peer in range(PEERS):
        send_ref[peer, :, :WIDTH] = back[PORTION * peer : PORTION * (peer + 1)]


def pieces_kernel(scal_ref, got_ref, out_ref):
    total = got_ref[0, :, WIDTH:].astype(F32)
    for peer in range(1, PEERS):
        total = total + got_ref[peer, :, WIDTH:].astype(F32)
    turned = jnp.concatenate([total[:, HD:], total[:, :HD]], 1)
    total = jnp.where(scal_ref[5] == 1, turned, total)
    for k in range(PIECE // 128):
        out_ref[:, k, :] = total[:, k * 128 : (k + 1) * 128]
    out_ref[:, PIECE // 128 :, :] = jnp.zeros((16, 8 - PIECE // 128, 128), F32)


def unpack_kernel(slot_ref, rows_ref, out_ref):
    order = mark(iota((ROWS, ROWS), 0) == slot_ref[...])
    out_ref[...] = tn(order, rows_ref[:, :, :WIDTH].reshape(ROWS, WIDTH)).astype(BF)


class Late:
    def __init__(self, source, buffer, semaphore):
        self.buffer = buffer
        self.copy = pltpu.make_async_copy(source, buffer, semaphore)
        self.copy.start()
        self.ready = False

    def wait(self):
        if not self.ready:
            self.copy.wait()
            self.ready = True

    def __getitem__(self, index):
        self.wait()
        return self.buffer[index]


class Early:
    def __init__(self, target, buffer, semaphore):
        self.buffer = buffer
        self.copy = pltpu.make_async_copy(buffer, target, semaphore)
        self.sent = False

    def __setitem__(self, index, value):
        self.buffer[index] = value

    def send(self):
        if not self.sent:
            self.copy.start()
            self.sent = True


HERE, LATE, TIE, SCALAR = "here", "late", "tie", "scalar"
SPACES = {
    HERE: pl.BlockSpec(memory_space=pltpu.VMEM),
    TIE: pl.BlockSpec(memory_space=pl.ANY),
    SCALAR: pl.BlockSpec(memory_space=pltpu.SMEM),
}
FAR_AWAY = pl.BlockSpec(memory_space=pltpu.HBM)
QUERY = (0, ROWS, 0, INNER)
KEY_VALUE = (0, ROWS, INNER, 2 * INNER)
CODE = (0, ROWS, 3 * INNER, 128)
FAR_QUERY = (ROWS, FAR, 0, INNER)
FAR_GRAD = (ROWS, FAR, INNER, INNER)
MEAN = (0, FAR, 0, INNER + 128)
LEFT = ((6656, 3 * INNER + 128), BF, (QUERY, KEY_VALUE, CODE, FAR_QUERY, FAR_GRAD))
GRADS = ((21504, INNER), BF, (QUERY,))
ATTENTION = (0, ROWS, 3 * INNER + 128, INNER)
GRAD_QUERY = (0, ROWS, 0, INNER)
GRAD_KEY = (0, ROWS, 0, INNER)
GRAD_VALUE = (0, ROWS, INNER, INNER)
HELD_MEAN = (ROWS, FAR, 0, INNER + 128)
HELD16 = (
    (ROWS + FAR, 4 * INNER + 128),
    BF,
    (KEY_VALUE, CODE, FAR_QUERY, FAR_GRAD, ATTENTION, GRAD_QUERY),
)
HELD32 = ((ROWS + FAR, 2 * INNER), F32, (HELD_MEAN, GRAD_KEY, GRAD_VALUE))
MEANS = ((8320, INNER + 128), F32, (MEAN,))


def part(ref, window):
    if window == LATE:
        return ref
    return ref.at[pl.ds(window[0], window[1]), pl.ds(window[2], window[3])]


def scalars(lengths_ref):
    device = lax.axis_index("ctx")
    inner = device & 7
    length = lengths_ref[0]
    head = jnp.where(inner >= HEADS, inner - HEADS, inner)
    return (length - device * ROWS, length, device >> 3, head, inner, device & 1)


def call(body, name, flops, ins, outs, scratch=(), limit=LIMIT):
    staged = []
    for array, kind in ins:
        if kind not in SPACES:
            staged.append((array.shape if kind == LATE else (kind[1], kind[3]), array.dtype))
    for dims, dtype, kind in outs:
        if kind == LATE:
            staged.append((dims, dtype))
        elif kind not in SPACES:
            staged += [((w[1], w[3]), dtype) for w in kind]

    def kernel(*refs):
        refs = list(refs)
        operands = [refs.pop(0) for _ in ins]
        targets = [refs.pop(0) for _ in outs]
        buffers = [refs.pop(0) for _ in staged]
        semaphores = refs.pop(0) if staged else None
        at = 0
        for i, (_, kind) in enumerate(ins):
            if kind == SCALAR:
                operands[i] = scalars(operands[i])
            if kind not in SPACES:
                operands[i] = Late(part(operands[i], kind), buffers[at], semaphores.at[at])
                at += 1
        results = []
        for target, (_, _, kind) in zip(targets, outs):
            if kind in SPACES:
                results.append(target)
                continue
            for w in (LATE,) if kind == LATE else kind:
                results.append(Early(part(target, w), buffers[at], semaphores.at[at]))
                at += 1
        body(*operands, *results, *refs)
        for operand in operands:
            if isinstance(operand, Late):
                operand.wait()
        for result in results:
            if isinstance(result, Early):
                result.send()
        for result in results:
            if isinstance(result, Early):
                result.copy.wait()

    return pl.pallas_call(
        kernel,
        out_shape=[jax.ShapeDtypeStruct(dims, dtype) for dims, dtype, _ in outs],
        in_specs=[SPACES.get(kind, FAR_AWAY) for _, kind in ins],
        out_specs=[SPACES.get(kind, FAR_AWAY) for _, _, kind in outs],
        scratch_shapes=[pltpu.VMEM(dims, dtype) for dims, dtype in staged]
        + ([pltpu.SemaphoreType.DMA((len(staged),))] if staged else [])
        + list(scratch),
        name=name,
        compiler_params=pltpu.CompilerParams(vmem_limit_bytes=limit),
        cost_estimate=pl.CostEstimate(flops=flops, bytes_accessed=4_000_000, transcendentals=0),
    )(*[a for a, _ in ins])


def exchange(rows, axis):
    return lax.all_to_all(rows, axis, split_axis=0, concat_axis=0, tiled=True)


def local(tiles, tile_pos, lengths, qkv_weight, out_weight, cotangent):
    cot = cotangent[0]

    sent, slot = call(
        pack_kernel,
        "pack",
        800_000_000,
        [(tile_pos, LATE), (tiles[0], LATE)],
        [((ROWS, 896), BF, LATE), ((1, ROWS), jnp.int32, LATE)],
        limit=ALL,
    )
    got = exchange(sent.reshape(PEERS, PORTION, 896), "ctx").reshape(ROWS, 896)

    (grad_out,) = call(
        grad_kernel,
        "grad",
        400_000_000,
        [(lengths, SCALAR), (cot, LATE), (out_weight, LATE)],
        [GRADS],
    )

    far_sent, left, means = call(
        project_kernel,
        "project",
        3_000_000_000,
        [(lengths, SCALAR), (got, HERE), (qkv_weight, LATE), (grad_out, QUERY)],
        [((PEERS, CHUNK, 256), BF, LATE), LEFT, MEANS],
        limit=PROJECT_LIMIT,
    )
    far_got = exchange(far_sent, "ctx")

    held16, held32, after = call(
        local_kernel,
        "local_rows",
        12_000_000_000,
        [
            (lengths, SCALAR),
            (left, QUERY),
            (left, KEY_VALUE),
            (grad_out, QUERY),
            (left, CODE),
            (left, FAR_QUERY),
            (left, FAR_GRAD),
            (means, MEAN),
        ],
        [
            HELD16,
            HELD32,
            ((8320, 512), F32, ()),
        ],
        limit=LOCAL_LIMIT,
    )

    (far_back,) = call(
        far_kernel,
        "far",
        6_000_000_000,
        [(lengths, SCALAR), (far_got, HERE), (after, TIE)],
        [((8, CHUNK, 256), BF, HERE)],
        [pltpu.VMEM((KEYS, 128), F32)] * 4,
    )
    blocks = [[8 * b + j for j in range(8)] for b in range(PEERS // 8)]
    far_back = lax.all_to_all(
        far_back, "ctx", split_axis=0, concat_axis=0, axis_index_groups=blocks, tiled=True
    )

    back, pair = call(
        finish_kernel,
        "finish",
        4_000_000_000,
        [
            (lengths, SCALAR),
            (far_back, HERE),
            (held16, HERE),
            (held32, HERE),
            (cot, HERE),
            (qkv_weight, HERE),
        ],
        [((PEERS, PORTION, WIDTH + PIECE), BF, HERE), ((2, FAR, HD), F32, LATE)],
    )
    returned = exchange(back, "ctx")
    (pieces,) = call(
        pieces_kernel,
        "pieces",
        1_000_000,
        [(lengths, SCALAR), (returned, HERE)],
        [((16, 8, 128), F32, HERE)],
    )
    pieces = exchange(pieces, "slide")
    weight_grad = jnp.sum(pieces, 0).reshape(-1)[:576]
    (tile_grads,) = call(
        unpack_kernel, "unpack", 400_000_000, [(slot, LATE), (returned, HERE)], [((ROWS, WIDTH), BF, LATE)]
    )
    return (tile_grads[None], weight_grad, pair.reshape(1, 2, HEADS, GROUPS, HD))


def solution(mesh):
    placed = (
        P("slide", "ctx", None),
        P("slide", "ctx"),
        P("slide"),
        P(),
        P(),
        P("slide", "ctx", None),
    )
    return jax.shard_map(
        local,
        mesh=mesh,
        in_specs=placed,
        out_specs=(
            P("slide", "ctx", None),
            P(("slide", "ctx")),
            P("slide", None, None, "ctx", None),
        ),
        check_vma=False,
    )
```
